32 devices in a mesh: samp: 4 (over z), feat: 8 (over y, x, core).
Axes of the slice: x: 2, y: 2, z: 4, core: 2. Of those that a mesh axis runs over, the one named last changes fastest.
Arguments:
- inputs: bfloat16 [440, 8192], P(None, ('samp', 'feat')), may hold values from -6 to 6
- probs: bfloat16 [147, 8192], P(None, ('samp', 'feat')), may hold values from 0 to 1, as said below
- labels: int32 [8192], P(('samp', 'feat')), may hold values from 0 to 146
- proj_weight: bfloat16 [440, 32768], P(None, ('feat', 'samp')), may hold values from -0.25 to 0.25
- phase: bfloat16 [1, 32768], P(None, ('feat', 'samp')), may hold values from -3.140625 to 3.140625
- direction: bfloat16 [147, 32768], P(None, ('feat', 'samp')), may hold values from -0.03125 to 0.03125
- damping: float32 [1], replicated, may hold values from 300 to 3000
Outputs:
- hess_vec: float32 [147, 32768], P(None, ('feat', 'samp'))
- gradient: float32 [147, 32768], P(None, ('feat', 'samp'))
The draws below stay inside these ranges and needn't reach their ends.
Inputs may be any that keep to these rules, and one draw needn't show every extreme that they name: Each column of probs is positive and sums to one up to rounding.
All inputs are finite; a program needn't handle non-finite values.
Results may differ from the reference program's by a relative error of at most 0.005.
The reference program's roundings to bfloat16 on the way count: a program that leaves them out, or rounds other values in their place, can miss the bound.
Values may be sent and summed in bfloat16 or wider, within the bound.
No kernel may reach another device: no remote copies, remote signals or barrier semaphores. Data moves between devices by JAX's collectives and lax.ppermute only.
A program may use at most 64 MiB of HBM per device.

```python
import math
import jax
import jax.numpy as jnp
from jax import lax

RAW = 440
C = 147
F = 32768
SAMPLES = 8192


def draw_probs(key, part):
    key_top = jax.random.fold_in(key, 11)
    key_rest = jax.random.fold_in(key, 23)
    key_lift = jax.random.fold_in(key, 37)
    chosen = jax.random.randint(key_top, (1, SAMPLES), 0, C)
    class_ids = lax.broadcasted_iota(jnp.int32, (C, SAMPLES), 0)
    marked = (class_ids == chosen).astype(jnp.float32)
    base_lift = math.log(C - 1.0)
    rest = 0.3 * jax.random.normal(key_rest, (C, SAMPLES), jnp.float32)
    lift = base_lift + 1.0 + 0.0 * jax.random.uniform(key_lift, (1, SAMPLES), jnp.float32)
    logits = rest + lift * marked
    return jax.nn.softmax(logits, axis=0).astype(jnp.bfloat16)


def set_ends(values, key, least, largest):
    longest = values.shape.index(max(values.shape))
    spots = []
    for shift in (0, 1):
        where = [jax.random.randint(jax.random.fold_in(key, axis), (), 0, length) for axis, length in enumerate(values.shape)]
        where[longest] = (where[longest] + shift) % values.shape[longest]
        spots.append(tuple(where))
    return values.at[spots[0]].set(least).at[spots[1]].set(largest)


def levels(own_key, extent, shards, low, top_value):
    def one(axis_at, shards_of):
        steps = jax.random.uniform(jax.random.fold_in(jax.random.fold_in(own_key, 6), axis_at), (shards_of,), jnp.float32, low / len(shards), top_value / len(shards))
        return jnp.repeat(jnp.exp(steps), extent[axis_at] // shards_of).reshape((-1,) + (1,) * (len(extent) - axis_at - 1))

    level = one(*shards[0])
    for cut in shards[1:]:
        level = level * one(*cut)
    return level


def gaussian(own_key, extent, scale, limit, shards=(), held_as=jnp.bfloat16):
    result = scale * jax.random.normal(own_key, extent, jnp.float32)
    if shards:
        result = result * levels(own_key, extent, shards, -0.22, 0.18)
    return jnp.clip(result, -limit, limit).astype(held_as)


def setup_inputs(seed: int = 0) -> dict:
    key_of = jax.random.split(jax.random.key(seed), 8)
    inputs = gaussian(key_of[0], (RAW, SAMPLES), 1.0, 6.0, ((1, 32),))
    probs = draw_probs(jax.random.fold_in(key_of[7], 71), 0)
    labels = set_ends(jax.random.randint(key_of[2], (SAMPLES,), 0, C), jax.random.fold_in(key_of[2], 1), 0, C - 1).astype(jnp.int32)
    proj_weight = gaussian(key_of[3], (RAW, F), RAW ** -0.5, 0.25, ((1, 32),))
    phase = jnp.clip(jax.random.uniform(key_of[4], (1, F), jnp.float32, -3.140625, 3.140625), -3.140625, 3.140625).astype(jnp.bfloat16)
    direction = gaussian(key_of[5], (C, F), F ** -0.5, 0.03125, ((1, 32),))
    damping = jnp.clip(jnp.exp(jax.random.uniform(key_of[6], (1,), jnp.float32, math.log(300.0), math.log(3000.0))), 300.0, 3000.0)
    return {"inputs": inputs, "probs": probs, "labels": labels, "proj_weight": proj_weight, "phase": phase, "direction": direction, "damping": damping}


def reference(inputs, probs, labels, proj_weight, phase, direction, damping):
    block = min(1024, SAMPLES)
    count = SAMPLES // block
    x_blocks = inputs.reshape(RAW, count, block).transpose(1, 0, 2)
    p_blocks = probs.reshape(C, count, block).transpose(1, 0, 2)
    l_blocks = labels.reshape(count, block)
    phase_col = phase.astype(jnp.float32).T
    classes = lax.broadcasted_iota(jnp.int32, (C, block), 0)

    def step(carry, pieces):
        hv_acc, grad_acc = carry
        x_block, p_block, l_block = pieces
        proj = lax.dot_general(proj_weight, x_block, (((0,), (0,)), ((), ())), preferred_element_type=jnp.float32)
        feats = jnp.cos(proj + phase_col).astype(jnp.bfloat16)
        tangent = jnp.dot(direction, feats, preferred_element_type=jnp.float32)
        prob = p_block.astype(jnp.float32)
        mixed = jnp.sum(prob * tangent, axis=0, keepdims=True)
        curv = (prob * (tangent - mixed)).astype(jnp.bfloat16)
        onehot = (classes == l_block[None, :]).astype(jnp.float32)
        resid = (prob - onehot).astype(jnp.bfloat16)
        dims = (((1,), (1,)), ((), ()))
        hv_acc = hv_acc + lax.dot_general(curv, feats, dims, preferred_element_type=jnp.float32)
        grad_acc = grad_acc + lax.dot_general(resid, feats, dims, preferred_element_type=jnp.float32)
        return (hv_acc, grad_acc), None

    start = (jnp.zeros((C, F), jnp.float32), jnp.zeros((C, F), jnp.float32))
    (hv_acc, grad_acc), _ = lax.scan(step, start, (x_blocks, p_blocks, l_blocks))
    hess_vec = hv_acc + damping[0] * direction.astype(jnp.float32)
    return hess_vec, grad_acc
```

```python
import functools
import math

import jax
import jax.numpy as jnp
from jax import lax
from jax.experimental import pallas as pl
from jax.experimental.pallas import tpu as pltpu
from jax.sharding import PartitionSpec as P

F32, BF16 = jnp.float32, jnp.bfloat16
VMEM = 48 * 2**20
COEFS = (0.99999921, -19.73898036, 64.92865742, -85.27162153, 58.79049212, -21.07110563)
ROUNDER = 12582912.0


def up(value, step):
    return -(-value // step) * step


def params():
    return pltpu.CompilerParams(vmem_limit_bytes=VMEM)


def cosine(angle):
    turns = angle * (0.5 / math.pi)
    rest = turns - ((turns + ROUNDER) - ROUNDER)
    square = rest * rest
    total = square * COEFS[-1] + COEFS[-2]
    for coef in COEFS[-3::-1]:
        total = total * square + coef
    return total


def pack_kernel(raw, classes, x_ref, p_ref, l_ref, w_ref, ph_ref, d_ref, xo_ref, wo_ref):
    depth = up(raw + 1, 16)
    rows = xo_ref.shape[0]
    n, f = xo_ref.shape[1], wo_ref.shape[1]
    xo_ref[:raw, :] = x_ref[...]
    first = lax.broadcasted_iota(jnp.int32, (depth - raw, n), 0) == 0
    xo_ref[raw:depth, :] = jnp.where(first, 1.0, 0.0).astype(BF16)
    ids = lax.broadcasted_iota(jnp.int32, (classes, n), 0)
    onehot = (ids == l_ref[...]).astype(F32)
    xo_ref[depth : depth + classes, :] = (p_ref[...].astype(F32) - onehot).astype(BF16)
    xo_ref[depth + classes :, :] = jnp.zeros((rows - depth - classes, n), BF16)
    wo_ref[:raw, :] = w_ref[...]
    head = lax.broadcasted_iota(jnp.int32, (depth - raw, f), 0) == 0
    wo_ref[raw:depth, :] = jnp.where(head, ph_ref[...].astype(F32), 0.0).astype(BF16)
    wo_ref[depth : depth + classes, :] = d_ref[...]
    wo_ref[depth + classes :, :] = jnp.zeros((rows - depth - classes, f), BF16)


def turn_kernel(depth, *refs):
    count = len(refs) - 2
    xt_ref, r_ref = refs[count:]
    n = refs[0].shape[1]
    for j in range(count):
        xt_ref[j * n : (j + 1) * n, :] = refs[j][:depth, :].T
        r_ref[:, j * n : (j + 1) * n] = refs[j][depth:, :]


def feature_kernel(depth, cuts, has_total, last, half, xt_ref, *refs):
    refs = list(refs)
    w_refs = [refs.pop(0) for _ in cuts]
    t_ref = refs.pop(0) if has_total else None
    f_ref = refs.pop(0)
    proj, spot = None, 0
    for w_ref in w_refs:
        end = min(spot + w_ref.shape[0], depth)
        part = jnp.dot(xt_ref[:, spot:end], w_ref[: end - spot, :], preferred_element_type=F32)
        proj = part if proj is None else proj + part
        spot += w_ref.shape[0]
    direction = w_refs[-1][w_refs[-1].shape[0] - (spot - depth) :, :]
    feats = cosine(proj).astype(BF16)
    f_ref[...] = feats
    tangent = lax.dot_general(feats, direction, (((1,), (1,)), ((), ())), preferred_element_type=F32)
    if has_total:
        tangent = tangent + t_ref[...]
    if not last:
        refs[0][...] = tangent
    else:
        other_ref, own_ref = refs
        step = pl.program_id(0)

        @pl.when(step < half)
        def _():
            other_ref[...] = tangent.T.astype(BF16)

        @pl.when(step >= half)
        def _():
            own_ref[...] = tangent.T


def make_features(xt, ws, depth, total, last, block):
    n, f = xt.shape[0], ws[0].shape[1]
    wide = sum(w.shape[0] for w in ws) - depth
    steps = n // block
    half = steps // 2
    ins = [pl.BlockSpec((block, depth), lambda i: (i, 0))]
    ins += [pl.BlockSpec(w.shape, lambda i: (0, 0)) for w in ws]
    args = [xt, *ws]
    if total is not None:
        ins.append(pl.BlockSpec((block, wide), lambda i: (i, 0)))
        args.append(total)
    outs = [pl.BlockSpec((block, f), lambda i: (i, 0))]
    shapes = [jax.ShapeDtypeStruct((n, f), BF16)]
    if last:
        outs.append(pl.BlockSpec((wide, block), lambda i: (0, jnp.minimum(i, half - 1))))
        outs.append(pl.BlockSpec((wide, block), lambda i: (0, jnp.maximum(i - half, 0))))
        shapes.append(jax.ShapeDtypeStruct((wide, n // 2), BF16))
        shapes.append(jax.ShapeDtypeStruct((wide, n // 2), F32))
    else:
        outs.append(pl.BlockSpec((block, wide), lambda i: (i, 0)))
        shapes.append(jax.ShapeDtypeStruct((n, wide), F32))
    cost = pl.CostEstimate(flops=2 * n * f * (depth + wide), bytes_accessed=2 * n * f, transcendentals=0)
    return pl.pallas_call(
        functools.partial(feature_kernel, depth, [w.shape for w in ws], total is not None, last, half),
        grid=(steps,),
        in_specs=ins,
        out_specs=outs,
        out_shape=shapes,
        compiler_params=params(),
        cost_estimate=cost,
    )(*args)


def spread_kernel(own_ref, got_ref, keep_ref, *send_refs):
    n = keep_ref.shape[1]
    total = own_ref[...] + got_ref[...].astype(F32)
    keep_ref[...] = total[:, :n]
    for j, ref in enumerate(send_refs):
        ref[...] = total[:, (j + 1) * n : (j + 2) * n].astype(BF16)


def curve_kernel(classes, keep_ref, *refs):
    got_refs, p_ref, c_ref = refs[:-2], refs[-2], refs[-1]
    total = keep_ref[...]
    for ref in got_refs:
        total = total + ref[...].astype(F32)
    total = total[:classes, :]
    prob = p_ref[...].astype(F32)
    mixed = jnp.sum(prob * total, axis=0, keepdims=True)
    c_ref[:classes, :] = (prob * (total - mixed)).astype(BF16)
    c_ref[classes:, :] = jnp.zeros((c_ref.shape[0] - classes, c_ref.shape[1]), BF16)


def share_kernel(*refs):
    left_refs, f_ref, o_ref = refs[:-2], refs[-2], refs[-1]
    total, spot = None, 0
    for ref in left_refs:
        n = ref.shape[1]
        part = jnp.dot(ref[...], f_ref[spot : spot + n, :], preferred_element_type=F32)
        total = part if total is None else total + part
        spot += n
    o_ref[...] = total.astype(o_ref.dtype)


def make_share(lefts, feats, dtype, tile):
    n, f = feats.shape
    wide = lefts[0].shape[0]
    return pl.pallas_call(
        share_kernel,
        grid=(f // tile,),
        in_specs=[pl.BlockSpec(a.shape, lambda i: (0, 0)) for a in lefts]
        + [pl.BlockSpec((n, tile), lambda i: (0, i))],
        out_specs=pl.BlockSpec((wide, tile), lambda i: (0, i)),
        out_shape=jax.ShapeDtypeStruct((wide, f), dtype),
        compiler_params=params(),
        cost_estimate=pl.CostEstimate(flops=2 * n * f * wide, bytes_accessed=2 * n * f, transcendentals=0),
    )(*lefts, feats)


def whole(kernel, shapes, *args):
    return pl.pallas_call(kernel, out_shape=shapes, compiler_params=params())(*args)


def on_device(line, ys, xs, inputs, probs, labels, proj_weight, phase, direction, damping):
    raw, own = inputs.shape
    classes = probs.shape[0]
    width = proj_weight.shape[1]
    depth = up(raw + 1, 16)
    wide = up(classes, 8)

    def swap_core(a):
        return lax.ppermute(a, "feat", [(i, i ^ 1) for i in range(2 * xs * ys)])

    def along(a, k):
        return lax.ppermute(a, "samp", [(i, (i + k) % line) for i in range(line)])

    def across(a, dy, dx):
        def to(i):
            y, x, c = i // (2 * xs), i // 2 % xs, i % 2
            return ((y + dy) % ys * xs + (x + dx) % xs) * 2 + c

        return lax.ppermute(a, "feat", [(i, to(i)) for i in range(2 * xs * ys)])

    offsets = [(dy, dx) for dy in range(ys) for dx in range(xs)]
    x_own, w_own = whole(
        functools.partial(pack_kernel, raw, classes),
        [jax.ShapeDtypeStruct((depth + wide, own), BF16), jax.ShapeDtypeStruct((depth + wide, width), BF16)],
        inputs, probs, labels[None, :], proj_weight, phase, direction,
    )
    x_line = [x_own] + [along(x_own, k) for k in range(1, line)]
    x_peer = [swap_core(a) for a in x_line]
    cut = up(depth // 2, 128)
    ws = {(0, 0): [w_own]}
    for dy in range(1, ys):
        ws[dy, 0] = [across(w_own, dy, 0)]
    for dx in range(1, xs):
        ws[0, dx] = [across(w_own, 0, dx)]
    for dy in range(1, ys):
        for dx in range(1, xs):
            ws[dy, dx] = [across(ws[0, dx][0][:cut], dy, 0), across(ws[dy, 0][0][cut:], 0, dx)]

    blocks = x_peer + x_line
    samples = own * len(blocks)
    xt, resid = whole(
        functools.partial(turn_kernel, depth),
        [jax.ShapeDtypeStruct((samples, depth), BF16), jax.ShapeDtypeStruct((wide, samples), BF16)],
        *blocks,
    )
    feats, total = {}, None
    for at in offsets:
        last = at == offsets[-1]
        feats[at], *rest = make_features(xt, ws[at], depth, total, last, own)
        total = rest[0]
    t_other, t_own = rest
    t_got = swap_core(t_other)
    keep, *send = whole(
        spread_kernel,
        [jax.ShapeDtypeStruct((wide, own), F32)] + [jax.ShapeDtypeStruct((wide, own), BF16)] * (line - 1),
        t_own, t_got,
    )
    got = [along(a, -k) for k, a in enumerate(send, 1)]
    curv = whole(
        functools.partial(curve_kernel, classes), jax.ShapeDtypeStruct((wide, own), BF16), keep, *got, probs
    )
    c_line = [curv] + [along(curv, k) for k in range(1, line)]
    c_peer = [swap_core(a) for a in c_line]
    curvs = c_peer + c_line

    def reduce(lefts):
        out = None
        for dy, dx in offsets[:0:-1]:
            piece = across(make_share(lefts, feats[dy, dx], BF16, width // 2), -dy, -dx).astype(F32)
            out = piece if out is None else out + piece
        own_part = make_share(lefts, feats[0, 0], F32, width // 2)
        return (own_part + out if out is not None else own_part)[:classes]

    gradient = reduce([resid])
    hess_vec = reduce(curvs) + damping[0] * direction.astype(F32)
    return (hess_vec, gradient)


def solution(mesh):
    line, feat = mesh.shape["samp"], mesh.shape["feat"]
    ys = 2 if feat % 4 == 0 else 1
    xs = feat // (2 * ys)
    placed = (
        P(None, ("samp", "feat")),
        P(None, ("samp", "feat")),
        P(("samp", "feat")),
        P(None, ("feat", "samp")),
        P(None, ("feat", "samp")),
        P(None, ("feat", "samp")),
        P(),
    )
    return jax.shard_map(
        functools.partial(on_device, line, ys, xs),
        mesh=mesh,
        in_specs=placed,
        out_specs=(P(None, ("feat", "samp")), P(None, ("feat", "samp"))),
        check_vma=False,
    )
```

```python
import functools
import math

import jax
import jax.numpy as jnp
from jax import lax
from jax.experimental import pallas as pl
from jax.experimental.pallas import tpu as pltpu
from jax.sharding import PartitionSpec as P

F32, BF16 = jnp.float32, jnp.bfloat16
VMEM = 16 * 2**20
COEFS = (0.99999921, -19.73898036, 64.92865742, -85.27162153, 58.79049212, -21.07110563)
ROUNDER = 12582912.0


def up(value, step):
    return -(-value // step) * step


def params():
    return pltpu.CompilerParams(vmem_limit_bytes=VMEM)


def cosine(angle):
    turns = angle * (0.5 / math.pi)
    rest = turns - ((turns + ROUNDER) - ROUNDER)
    square = rest * rest
    total = square * COEFS[-1] + COEFS[-2]
    for coef in COEFS[-3::-1]:
        total = total * square + coef
    return total


def pack_weights_kernel(raw, depth, classes, w_ref, ph_ref, d_ref, o_ref):
    rows, f = o_ref.shape
    o_ref[:raw, :] = w_ref[...]
    head = lax.broadcasted_iota(jnp.int32, (depth - raw, f), 0) == 0
    o_ref[raw:depth, :] = jnp.where(head, ph_ref[...].astype(F32), 0.0).astype(BF16)
    o_ref[depth : depth + classes, :] = d_ref[...]
    o_ref[depth + classes :, :] = jnp.zeros((rows - depth - classes, f), BF16)


def pack_samples_kernel(raw, depth, classes, x_ref, p_ref, l_ref, o_ref):
    rows, n = o_ref.shape
    o_ref[:raw, :] = x_ref[...]
    head = lax.broadcasted_iota(jnp.int32, (depth - raw, n), 0) == 0
    o_ref[raw:depth, :] = jnp.where(head, 1.0, 0.0).astype(BF16)
    ids = lax.broadcasted_iota(jnp.int32, (classes, n), 0)
    onehot = (ids == l_ref[...]).astype(F32)
    o_ref[depth : depth + classes, :] = (p_ref[...].astype(F32) - onehot).astype(BF16)
    o_ref[depth + classes :, :] = jnp.zeros((rows - depth - classes, n), BF16)


def pack(kernel, shape, *args):
    return pl.pallas_call(
        kernel,
        grid=(1,),
        in_specs=[pl.BlockSpec(a.shape, lambda i: (0, 0)) for a in args],
        out_specs=pl.BlockSpec(shape, lambda i: (0, 0)),
        out_shape=jax.ShapeDtypeStruct(shape, BF16),
        compiler_params=params(),
    )(*args)


def one_block(xt, w_refs, depth):
    proj, spot = None, 0
    for w_ref in w_refs:
        end = min(spot + w_ref.shape[0], depth)
        part = jnp.dot(xt[:, spot:end], w_ref[: end - spot, :], preferred_element_type=F32)
        proj = part if proj is None else proj + part
        spot += w_ref.shape[0]
    direction = w_refs[-1][w_refs[-1].shape[0] - (spot - depth) :, :]
    feats = cosine(proj).astype(BF16)
    return feats, lax.dot_general(feats, direction, (((1,), (1,)), ((), ())), preferred_element_type=F32)


def first_kernel(depth, count, *refs):
    x_refs, w_ref = refs[:count], refs[count]
    xt_ref, f_ref, t_ref = refs[count + 1 :]
    n = x_refs[0].shape[1]
    for j in range(count):
        here = slice(j * n, (j + 1) * n)
        xt = x_refs[j][:depth, :].T
        xt_ref[here, :] = xt
        f_ref[here, :], t_ref[here, :] = one_block(xt, [w_ref], depth)


def next_kernel(depth, count, totals, pieces, block, last, *refs):
    refs = list(refs)
    xt_refs, t_refs = refs[:count], refs[count : count + totals]
    refs = refs[count + totals :]
    w_refs = [[refs.pop(0) for _ in range(k)] for k in pieces]
    f_refs = [refs.pop(0) for _ in pieces]
    spot = 0
    t_blocks = [(ref, at) for ref in t_refs for at in range(0, ref.shape[0], block)]
    for xt_ref in xt_refs:
        for at in range(0, xt_ref.shape[0], block):
            t_ref, t_at = t_blocks[spot // block]
            xt, total = xt_ref[at : at + block, :], t_ref[t_at : t_at + block, :]
            for ws, f_ref in zip(w_refs, f_refs, strict=True):
                f_ref[spot : spot + block, :], tangent = one_block(xt, ws, depth)
                total = total + tangent
            if not last:
                refs[0][spot : spot + block, :] = total
            else:
                pair, mine = spot // (2 * block), spot // block % 2
                here = slice(pair * block, (pair + 1) * block)
                if mine:
                    refs[1][:, here] = total.T
                else:
                    refs[0][:, here] = total.T.astype(BF16)
            spot += block


def make_next(xts, totals, pieces, depth, wide, block, last):
    n, f = sum(a.shape[0] for a in xts), pieces[0][0].shape[1]
    shapes = [jax.ShapeDtypeStruct((n, f), BF16)] * len(pieces)
    if last:
        shapes.append(jax.ShapeDtypeStruct((wide, n // 2), BF16))
        shapes.append(jax.ShapeDtypeStruct((wide, n // 2), F32))
    else:
        shapes.append(jax.ShapeDtypeStruct((n, wide), F32))
    kernel = functools.partial(next_kernel, depth, len(xts), len(totals), [len(ws) for ws in pieces], block, last)
    out = whole(kernel, shapes, *xts, *totals, *[w for ws in pieces for w in ws], flops=2 * n * f * len(pieces) * (depth + wide))
    return out[: len(pieces)], out[len(pieces) :]


def spread_kernel(own_ref, got_ref, keep_ref, *send_refs):
    n = keep_ref.shape[1]
    total = own_ref[...] + got_ref[...].astype(F32)
    keep_ref[...] = total[:, :n]
    for j, ref in enumerate(send_refs):
        ref[...] = total[:, (j + 1) * n : (j + 2) * n].astype(BF16)


def curve_kernel(classes, keep_ref, *refs):
    got_refs, p_ref, c_ref = refs[:-2], refs[-2], refs[-1]
    total = keep_ref[...]
    for ref in got_refs:
        total = total + ref[...].astype(F32)
    total = total[:classes, :]
    prob = p_ref[...].astype(F32)
    mixed = jnp.sum(prob * total, axis=0, keepdims=True)
    c_ref[:classes, :] = (prob * (total - mixed)).astype(BF16)
    c_ref[classes:, :] = jnp.zeros((c_ref.shape[0] - classes, c_ref.shape[1]), BF16)


def share_kernel(count, skip, block, *refs):
    left_refs, f_refs, o_ref = refs[:count], refs[count:-1], refs[-1]
    f_blocks = [(ref, at) for ref in f_refs for at in range(0, ref.shape[0], block)]
    total = None
    for left_ref, (f_ref, at) in zip(left_refs, f_blocks, strict=True):
        part = jnp.dot(left_ref[skip:, :], f_ref[at : at + block, :], preferred_element_type=F32)
        total = part if total is None else total + part
    o_ref[...] = total.astype(o_ref.dtype)


def make_share(lefts, skip, feats, dtype):
    block = lefts[0].shape[1]
    wide, n, f = lefts[0].shape[0] - skip, sum(a.shape[0] for a in feats), feats[0].shape[1]
    return whole(
        functools.partial(share_kernel, len(lefts), skip, block),
        jax.ShapeDtypeStruct((wide, f), dtype),
        *lefts, *feats, flops=2 * n * f * wide,
    )


def whole(kernel, shapes, *args, flops=0):
    size = sum(math.prod(a.shape) * a.dtype.itemsize for a in args)
    cost = pl.CostEstimate(flops=flops, bytes_accessed=size, transcendentals=0)
    return pl.pallas_call(kernel, out_shape=shapes, compiler_params=params(), cost_estimate=cost)(*args)


def on_device(line, ys, xs, inputs, probs, labels, proj_weight, phase, direction, damping):
    raw, own = inputs.shape
    classes = probs.shape[0]
    width = proj_weight.shape[1]
    depth = up(raw + 1, 16)
    wide = up(classes, 8)

    def swap_core(a):
        return lax.ppermute(a, "feat", [(i, i ^ 1) for i in range(2 * xs * ys)])

    def along(a, k):
        return lax.ppermute(a, "samp", [(i, (i + k) % line) for i in range(line)])

    def across(a, dy, dx):
        def to(i):
            y, x, c = i // (2 * xs), i // 2 % xs, i % 2
            return ((y + dy) % ys * xs + (x + dx) % xs) * 2 + c

        return lax.ppermute(a, "feat", [(i, to(i)) for i in range(2 * xs * ys)])

    offsets = [(dy, dx) for dy in range(ys) for dx in range(xs)]
    w_own = pack(
        functools.partial(pack_weights_kernel, raw, depth, classes), (depth + wide, width), proj_weight, phase, direction
    )
    ws = {(0, 0): [w_own]}
    for dy in range(1, ys):
        ws[dy, 0] = [across(w_own, dy, 0)]
    for dx in range(1, xs):
        ws[0, dx] = [across(w_own, 0, dx)]
    x_own = pack(
        functools.partial(pack_samples_kernel, raw, depth, classes), (depth + wide, own), inputs, probs, labels[None, :]
    )
    x_line = [x_own] + [along(x_own, k) for k in range(1, line)]
    blocks = [b for a in x_line for b in (swap_core(a), a)]
    cut = up(depth // 2, 128)
    for dy in range(1, ys):
        for dx in range(1, xs):
            ws[dy, dx] = [across(ws[0, dx][0][:cut], dy, 0), across(ws[dy, 0][0][cut:], 0, dx)]

    feats = {(0, 0): []}
    xts, totals = [], []
    for k in range(line):
        pair = 2 * own
        xt, part, total = whole(
            functools.partial(first_kernel, depth, 2),
            [
                jax.ShapeDtypeStruct((pair, depth), BF16),
                jax.ShapeDtypeStruct((pair, width), BF16),
                jax.ShapeDtypeStruct((pair, wide), F32),
            ],
            *blocks[2 * k : 2 * k + 2], w_own, flops=2 * pair * width * (depth + wide),
        )
        xts.append(xt)
        totals.append(total)
        feats[0, 0].append(part)
    near = [at for at in offsets[1:] if 0 in at]
    far = [at for at in offsets[1:] if 0 not in at]
    groups = [group for group in (near, far) if group]
    for group in groups:
        got, rest = make_next(xts, totals, [ws[at] for at in group], depth, wide, own, group is groups[-1])
        for at, piece in zip(group, got, strict=True):
            feats[at] = [piece]
        if group is not groups[-1]:
            totals = [rest[0]]
    t_other, t_own = rest
    t_got = swap_core(t_other)
    keep, *send = whole(
        spread_kernel,
        [jax.ShapeDtypeStruct((wide, own), F32)] + [jax.ShapeDtypeStruct((wide, own), BF16)] * (line - 1),
        t_own, t_got,
    )
    got = [along(a, -k) for k, a in enumerate(send, 1)]

    def collect(parts):
        out = parts[0, 0]
        for dy, dx in offsets[1:]:
            out = out + across(parts[dy, dx], -dy, -dx).astype(F32)
        return out[:classes]

    parts = {at: make_share(blocks, depth, feats[at], F32 if at == (0, 0) else BF16) for at in offsets[::-1]}
    keep, parts = lax.optimization_barrier((keep, parts))
    gradient = collect(parts)
    curv = whole(
        functools.partial(curve_kernel, classes), jax.ShapeDtypeStruct((wide, own), BF16), keep, *got, probs
    )
    c_line = [curv] + [along(curv, k) for k in range(1, line)]
    curvs = [b for a in c_line for b in (swap_core(a), a)]

    hess_parts = {at: make_share(curvs, 0, feats[at], F32 if at == (0, 0) else BF16) for at in offsets[::-1]}
    hess_vec = collect(hess_parts) + damping[0] * direction.astype(F32)
    return (hess_vec, gradient)


def solution(mesh):
    line, feat = mesh.shape["samp"], mesh.shape["feat"]
    ys = 2 if feat % 4 == 0 else 1
    xs = feat // (2 * ys)
    placed = (
        P(None, ("samp", "feat")),
        P(None, ("samp", "feat")),
        P(("samp", "feat")),
        P(None, ("feat", "samp")),
        P(None, ("feat", "samp")),
        P(None, ("feat", "samp")),
        P(),
    )
    return jax.shard_map(
        functools.partial(on_device, line, ys, xs),
        mesh=mesh,
        in_specs=placed,
        out_specs=(P(None, ("feat", "samp")), P(None, ("feat", "samp"))),
        check_vma=False,
    )
```

```python
import functools
import math

import jax
import jax.numpy as jnp
from jax import lax
from jax.experimental import pallas as pl
from jax.experimental.pallas import tpu as pltpu
from jax.sharding import PartitionSpec as P

F32, BF16 = jnp.float32, jnp.bfloat16
VMEM = 16 * 2**20
COEFS = (0.99999921, -19.73898036, 64.92865742, -85.27162153, 58.79049212, -21.07110563)
ROUNDER = 12582912.0


def up(value, step):
    return -(-value // step) * step


def params():
    return pltpu.CompilerParams(vmem_limit_bytes=VMEM)


def cosine(angle):
    turns = angle * (0.5 / math.pi)
    rest = turns - ((turns + ROUNDER) - ROUNDER)
    square = rest * rest
    total = square * COEFS[-1] + COEFS[-2]
    for coef in COEFS[-3::-1]:
        total = total * square + coef
    return total


def fetch(refs, bufs, sems):
    copies = [pltpu.make_async_copy(ref, buf, sems.at[j]) for j, (ref, buf) in enumerate(zip(refs, bufs, strict=True))]
    for copy in copies:
        copy.start()
    for copy in copies:
        copy.wait()


def pack_weights_kernel(raw, depth, classes, w_hbm, ph_hbm, d_hbm, *refs):
    o_refs, (w_ref, ph_ref, d_ref, sems) = refs[:-4], refs[-4:]
    fetch((w_hbm, ph_hbm, d_hbm), (w_ref, ph_ref, d_ref), sems)
    rows, f = o_refs[0].shape
    for j, o_ref in enumerate(o_refs):
        here = slice(j * f, (j + 1) * f)
        o_ref[:raw, :] = w_ref[:, here]
        head = lax.broadcasted_iota(jnp.int32, (depth - raw, f), 0) == 0
        o_ref[raw:depth, :] = jnp.where(head, ph_ref[:, here].astype(F32), 0.0).astype(BF16)
        o_ref[depth : depth + classes, :] = d_ref[:, here]
        o_ref[depth + classes :, :] = jnp.zeros((rows - depth - classes, f), BF16)


def pack_samples_kernel(raw, depth, classes, x_hbm, p_hbm, l_hbm, o_ref, x_ref, p_ref, l_ref, sems):
    fetch((x_hbm, p_hbm, l_hbm), (x_ref, p_ref, l_ref), sems)
    rows, n = o_ref.shape
    o_ref[:raw, :] = x_ref[...]
    head = lax.broadcasted_iota(jnp.int32, (depth - raw, n), 0) == 0
    o_ref[raw:depth, :] = jnp.where(head, 1.0, 0.0).astype(BF16)
    ids = lax.broadcasted_iota(jnp.int32, (classes, n), 0)
    onehot = (ids == l_ref[...]).astype(F32)
    o_ref[depth : depth + classes, :] = (p_ref[...].astype(F32) - onehot).astype(BF16)
    o_ref[depth + classes :, :] = jnp.zeros((rows - depth - classes, n), BF16)


def pack(kernel, shapes, *args):
    return pl.pallas_call(
        kernel,
        in_specs=[pl.BlockSpec(memory_space=pl.ANY)] * len(args),
        out_shape=shapes,
        scratch_shapes=[pltpu.VMEM(a.shape, a.dtype) for a in args] + [pltpu.SemaphoreType.DMA((len(args),))],
        compiler_params=params(),
    )(*args)


def one_block(xt, w_ref, depth):
    feats = cosine(jnp.dot(xt, w_ref[:depth, :], preferred_element_type=F32)).astype(BF16)
    dims = (((1,), (1,)), ((), ()))
    return feats, lax.dot_general(feats, w_ref[depth:, :], dims, preferred_element_type=F32)


def first_kernel(depth, count, parts, *refs):
    x_refs, w_refs = refs[:count], refs[count : count + parts]
    xt_ref, t_ref, *f_refs = refs[count + parts :]
    n = x_refs[0].shape[1]
    for j in range(count):
        here = slice(j * n, (j + 1) * n)
        xt = x_refs[j][:depth, :].T
        xt_ref[here, :] = xt
        total = None
        for w_ref, f_ref in zip(w_refs, f_refs, strict=True):
            f_ref[here, :], tangent = one_block(xt, w_ref, depth)
            total = tangent if total is None else total + tangent
        t_ref[here, :] = total


def next_kernel(depth, count, totals, parts, block, last, *refs):
    xt_refs, t_refs = refs[:count], refs[count : count + totals]
    refs = refs[count + totals :]
    w_refs, f_refs, out_refs = refs[:parts], refs[parts : 2 * parts], refs[2 * parts :]
    t_blocks = [(ref, at) for ref in t_refs for at in range(0, ref.shape[0], block)]
    spot = 0
    for xt_ref in xt_refs:
        for at in range(0, xt_ref.shape[0], block):
            t_ref, t_at = t_blocks[spot // block]
            xt, total = xt_ref[at : at + block, :], t_ref[t_at : t_at + block, :]
            for w_ref, f_ref in zip(w_refs, f_refs, strict=True):
                f_ref[spot : spot + block, :], tangent = one_block(xt, w_ref, depth)
                total = total + tangent
            if not last:
                out_refs[0][spot : spot + block, :] = total
            else:
                pair, mine = spot // (2 * block), spot // block % 2
                here = slice(pair * block, (pair + 1) * block)
                if mine:
                    out_refs[1][:, here] = total.T
                else:
                    out_refs[0][:, here] = total.T.astype(BF16)
            spot += block


def make_next(xts, totals, pieces, depth, wide, block, last):
    n, f = sum(a.shape[0] for a in xts), pieces[0].shape[1]
    shapes = [jax.ShapeDtypeStruct((n, f), BF16)] * len(pieces)
    if last:
        shapes.append(jax.ShapeDtypeStruct((wide, n // 2), BF16))
        shapes.append(jax.ShapeDtypeStruct((wide, n // 2), F32))
    else:
        shapes.append(jax.ShapeDtypeStruct((n, wide), F32))
    kernel = functools.partial(next_kernel, depth, len(xts), len(totals), len(pieces), block, last)
    out = whole(kernel, shapes, *xts, *totals, *pieces, flops=2 * n * f * len(pieces) * (depth + wide))
    return out[: len(pieces)], out[len(pieces) :]


def spread_kernel(own_ref, got_ref, keep_ref, *send_refs):
    n = keep_ref.shape[1]
    total = own_ref[...] + got_ref[...].astype(F32)
    keep_ref[...] = total[:, :n]
    for j, ref in enumerate(send_refs):
        ref[...] = total[:, (j + 1) * n : (j + 2) * n].astype(BF16)


def curve_kernel(classes, keep_ref, *refs):
    got_refs, p_ref, c_ref = refs[:-2], refs[-2], refs[-1]
    total = keep_ref[...]
    for ref in got_refs:
        total = total + ref[...].astype(F32)
    total = total[:classes, :]
    prob = p_ref[...].astype(F32)
    mixed = jnp.sum(prob * total, axis=0, keepdims=True)
    c_ref[:classes, :] = (prob * (total - mixed)).astype(BF16)
    c_ref[classes:, :] = jnp.zeros((c_ref.shape[0] - classes, c_ref.shape[1]), BF16)


def share_kernel(count, skip, block, halves, *refs):
    left_refs, f_refs, o_ref = refs[:count], refs[count:-1], refs[-1]
    each = len(f_refs) // halves
    f = f_refs[0].shape[1]
    for h in range(halves):
        f_blocks = [(ref, at) for ref in f_refs[h * each : (h + 1) * each] for at in range(0, ref.shape[0], block)]
        total = None
        for left_ref, (f_ref, at) in zip(left_refs, f_blocks, strict=True):
            part = jnp.dot(left_ref[skip:, :], f_ref[at : at + block, :], preferred_element_type=F32)
            total = part if total is None else total + part
        o_ref[:, h * f : (h + 1) * f] = total.astype(o_ref.dtype)


def make_share(lefts, skip, feats, dtype):
    block = lefts[0].shape[1]
    wide, n, f = lefts[0].shape[0] - skip, block * len(lefts), sum(h[0].shape[1] for h in feats)
    return whole(
        functools.partial(share_kernel, len(lefts), skip, block, len(feats)),
        jax.ShapeDtypeStruct((wide, f), dtype),
        *lefts, *[a for h in feats for a in h], flops=2 * n * f * wide,
    )


def whole(kernel, shapes, *args, flops=0):
    size = sum(math.prod(a.shape) * a.dtype.itemsize for a in args)
    cost = pl.CostEstimate(flops=flops, bytes_accessed=size, transcendentals=0)
    return pl.pallas_call(kernel, out_shape=shapes, compiler_params=params(), cost_estimate=cost)(*args)


def on_device(line, ys, xs, inputs, probs, labels, proj_weight, phase, direction, damping):
    raw, own = inputs.shape
    classes = probs.shape[0]
    width = proj_weight.shape[1]
    depth = up(raw + 1, 16)
    wide = up(classes, 8)

    def swap_core(a):
        return lax.ppermute(a, "feat", [(i, i ^ 1) for i in range(2 * xs * ys)])

    def along(a, k):
        return lax.ppermute(a, "samp", [(i, (i + k) % line) for i in range(line)])

    def across(a, dy, dx):
        def to(i):
            y, x, c = i // (2 * xs), i // 2 % xs, i % 2
            return ((y + dy) % ys * xs + (x + dx) % xs) * 2 + c

        return lax.ppermute(a, "feat", [(i, to(i)) for i in range(2 * xs * ys)])

    offsets = [(dy, dx) for dy in range(ys) for dx in range(xs)]
    rows, half = depth + wide, width // 2
    w_own = pack(
        functools.partial(pack_weights_kernel, raw, depth, classes),
        [jax.ShapeDtypeStruct((rows, half), BF16)] * 2,
        proj_weight, phase, direction,
    )
    ws = {(0, 0): w_own}
    for h in (0, 1):
        for dx in range(1, xs):
            ws[0, dx, h] = across(w_own[h], 0, dx)
        for dy in range(1, ys):
            ws[dy, 0, 1 - h] = across(w_own[1 - h], dy, 0)
    for dy in range(1, ys):
        for dx in range(1, xs):
            ws[dy, dx, 0] = across(ws[0, dx, 0], dy, 0)
            ws[dy, dx, 1] = across(ws[dy, 0, 1], 0, dx)
    x_own = pack(
        functools.partial(pack_samples_kernel, raw, depth, classes),
        jax.ShapeDtypeStruct((rows, own), BF16),
        inputs, probs, labels[None, :],
    )
    x_line = [x_own] + [along(x_own, k) for k in range(1, line)]

    feats = {at: [[], []] for at in offsets}
    xts, totals, blocks = [], [], []
    for k in range(line):
        pair = 2 * own
        blocks += [swap_core(x_line[k]), x_line[k]]
        xt, total, *part = whole(
            functools.partial(first_kernel, depth, 2, 2),
            [jax.ShapeDtypeStruct((pair, depth), BF16), jax.ShapeDtypeStruct((pair, wide), F32)]
            + [jax.ShapeDtypeStruct((pair, half), BF16)] * 2,
            *blocks[-2:], *w_own, flops=2 * pair * width * (depth + wide),
        )
        xts.append(xt)
        totals.append(total)
        for h in (0, 1):
            feats[0, 0][h].append(part[h])
        if k + 1 < line:
            x_line[k + 1], totals[k] = lax.optimization_barrier((x_line[k + 1], totals[k]))
    soon = [(0, dx, 0) for dx in range(1, xs)] + [(dy, 0, 1) for dy in range(1, ys)]
    near = [(0, dx, 1) for dx in range(1, xs)] + [(dy, 0, 0) for dy in range(1, ys)]
    far = [(dy, dx, h) for dy in range(1, ys) for dx in range(1, xs) for h in (0, 1)]
    groups = [group for group in (soon, near, far) if group]
    for group in groups:
        last = group is groups[-1]
        got, rest = make_next(xts, totals, [ws[at] for at in group], depth, wide, own, last)
        for (dy, dx, h), piece in zip(group, got, strict=True):
            feats[dy, dx][h] = [piece]
        if not last:
            totals = rest
    t_other, t_own = rest
    t_got = swap_core(t_other)
    keep, *send = whole(
        spread_kernel,
        [jax.ShapeDtypeStruct((wide, own), F32)] + [jax.ShapeDtypeStruct((wide, own), BF16)] * (line - 1),
        t_own, t_got,
    )
    got = [along(a, -k) for k, a in enumerate(send, 1)]

    def collect(parts):
        out = parts[0, 0]
        for dy, dx in offsets[1:]:
            out = out + parts[dy, dx].astype(F32)
        return out[:classes]

    def send_home(lefts, skip):
        parts = {at: make_share(lefts, skip, feats[at], F32 if at == (0, 0) else BF16) for at in offsets[::-1]}
        return parts, {(dy, dx): across(parts[dy, dx], -dy, -dx) for dy, dx in offsets[1:]}

    parts, arrived = send_home(blocks, depth)
    keep, parts = lax.optimization_barrier((keep, parts))
    curv = whole(
        functools.partial(curve_kernel, classes), jax.ShapeDtypeStruct((wide, own), BF16), keep, *got, probs
    )
    c_line = [curv] + [along(curv, k) for k in range(1, line)]
    curvs = [b for a in c_line for b in (swap_core(a), a)]
    curvs, arrived = lax.optimization_barrier((curvs, arrived))
    gradient = collect({(0, 0): parts[0, 0], **arrived})
    parts, arrived = send_home(curvs, 0)
    hess_vec = collect({(0, 0): parts[0, 0], **arrived}) + damping[0] * direction.astype(F32)
    return (hess_vec, gradient)


def solution(mesh):
    line, feat = mesh.shape["samp"], mesh.shape["feat"]
    ys = 2 if feat % 4 == 0 else 1
    xs = feat // (2 * ys)
    placed = (
        P(None, ("samp", "feat")),
        P(None, ("samp", "feat")),
        P(("samp", "feat")),
        P(None, ("feat", "samp")),
        P(None, ("feat", "samp")),
        P(None, ("feat", "samp")),
        P(),
    )
    return jax.shard_map(
        functools.partial(on_device, line, ys, xs),
        mesh=mesh,
        in_specs=placed,
        out_specs=(P(None, ("feat", "samp")), P(None, ("feat", "samp"))),
        check_vma=False,
    )
```

```python
import functools
import math

import jax
import jax.numpy as jnp
from jax import lax
from jax.experimental import pallas as pl
from jax.experimental.pallas import tpu as pltpu
from jax.sharding import PartitionSpec as P

F32, BF16 = jnp.float32, jnp.bfloat16
VMEM = 16 * 2**20
COEFS = (0.99999921, -19.73898036, 64.92865742, -85.27162153, 58.79049212, -21.07110563)
ROUNDER = 12582912.0


def up(value, step):
    return -(-value // step) * step


def params():
    return pltpu.CompilerParams(vmem_limit_bytes=VMEM)


def cosine(angle):
    turns = angle * (0.5 / math.pi)
    rest = turns - ((turns + ROUNDER) - ROUNDER)
    square = rest * rest
    total = square * COEFS[-1] + COEFS[-2]
    for coef in COEFS[-3::-1]:
        total = total * square + coef
    return total


def fetch(refs, bufs, sems):
    copies = [pltpu.make_async_copy(ref, buf, sems.at[j]) for j, (ref, buf) in enumerate(zip(refs, bufs, strict=True))]
    for copy in copies:
        copy.start()
    for copy in copies:
        copy.wait()


def pack_weights_kernel(raw, depth, classes, w_hbm, ph_hbm, d_hbm, *refs):
    o_refs, (w_ref, ph_ref, d_ref, sems) = refs[:-4], refs[-4:]
    fetch((w_hbm, ph_hbm, d_hbm), (w_ref, ph_ref, d_ref), sems)
    rows, f = o_refs[0].shape
    for j, o_ref in enumerate(o_refs):
        here = slice(j * f, (j + 1) * f)
        o_ref[:raw, :] = w_ref[:, here]
        head = lax.broadcasted_iota(jnp.int32, (depth - raw, f), 0) == 0
        o_ref[raw:depth, :] = jnp.where(head, ph_ref[:, here].astype(F32), 0.0).astype(BF16)
        o_ref[depth : depth + classes, :] = d_ref[:, here]
        o_ref[depth + classes :, :] = jnp.zeros((rows - depth - classes, f), BF16)


def pack_samples_kernel(raw, depth, classes, x_hbm, p_hbm, l_hbm, o_ref, x_ref, p_ref, l_ref, sems):
    fetch((x_hbm, p_hbm, l_hbm), (x_ref, p_ref, l_ref), sems)
    rows, n = o_ref.shape
    o_ref[:raw, :] = x_ref[...]
    head = lax.broadcasted_iota(jnp.int32, (depth - raw, n), 0) == 0
    o_ref[raw:depth, :] = jnp.where(head, 1.0, 0.0).astype(BF16)
    ids = lax.broadcasted_iota(jnp.int32, (classes, n), 0)
    onehot = (ids == l_ref[...]).astype(F32)
    o_ref[depth : depth + classes, :] = (p_ref[...].astype(F32) - onehot).astype(BF16)
    o_ref[depth + classes :, :] = jnp.zeros((rows - depth - classes, n), BF16)


def pack(kernel, shapes, *args):
    return pl.pallas_call(
        kernel,
        in_specs=[pl.BlockSpec(memory_space=pltpu.HBM)] * len(args),
        out_shape=shapes,
        scratch_shapes=[pltpu.VMEM(a.shape, a.dtype) for a in args] + [pltpu.SemaphoreType.DMA((len(args),))],
        compiler_params=params(),
    )(*args)


def one_block(xt, w_ref, depth):
    feats = cosine(jnp.dot(xt, w_ref[:depth, :], preferred_element_type=F32)).astype(BF16)
    dims = (((1,), (1,)), ((), ()))
    return feats, lax.dot_general(feats, w_ref[depth:, :], dims, preferred_element_type=F32)


def first_kernel(depth, count, parts, *refs):
    x_refs, w_refs = refs[:count], refs[count : count + parts]
    xt_ref, t_ref, *f_refs = refs[count + parts :]
    n = x_refs[0].shape[1]
    for j in range(count):
        here = slice(j * n, (j + 1) * n)
        xt = x_refs[j][:depth, :].T
        xt_ref[here, :] = xt
        total = None
        for w_ref, f_ref in zip(w_refs, f_refs, strict=True):
            f_ref[here, :], tangent = one_block(xt, w_ref, depth)
            total = tangent if total is None else total + tangent
        t_ref[here, :] = total


def next_kernel(depth, count, totals, parts, block, last, *refs):
    xt_refs, t_refs = refs[:count], refs[count : count + totals]
    refs = refs[count + totals :]
    w_refs, f_refs, out_refs = refs[:parts], refs[parts : 2 * parts], refs[2 * parts :]
    t_blocks = [(ref, at) for ref in t_refs for at in range(0, ref.shape[0], block)]
    spot = 0
    for xt_ref in xt_refs:
        for at in range(0, xt_ref.shape[0], block):
            t_ref, t_at = t_blocks[spot // block]
            xt, total = xt_ref[at : at + block, :], t_ref[t_at : t_at + block, :]
            for w_ref, f_ref in zip(w_refs, f_refs, strict=True):
                f_ref[spot : spot + block, :], tangent = one_block(xt, w_ref, depth)
                total = total + tangent
            if not last:
                out_refs[0][spot : spot + block, :] = total
            else:
                out_ref = out_refs[spot // out_refs[0].shape[1]]
                at_out = spot % out_ref.shape[1]
                out_ref[:, at_out : at_out + block] = total.T.astype(out_ref.dtype)
            spot += block


def make_next(xts, totals, pieces, depth, wide, block, last):
    n, f = sum(a.shape[0] for a in xts), pieces[0].shape[1]
    shapes = [jax.ShapeDtypeStruct((n, f), BF16)] * len(pieces)
    if last:
        shapes.append(jax.ShapeDtypeStruct((wide, n // 2), F32))
        shapes.append(jax.ShapeDtypeStruct((wide, n // 2), BF16))
    else:
        shapes.append(jax.ShapeDtypeStruct((n, wide), F32))
    kernel = functools.partial(next_kernel, depth, len(xts), len(totals), len(pieces), block, last)
    out = whole(kernel, shapes, *xts, *totals, *pieces, flops=2 * n * f * len(pieces) * (depth + wide))
    return out[: len(pieces)], out[len(pieces) :]


def spread_kernel(own_ref, got_ref, keep_ref, *send_refs):
    n = keep_ref.shape[1]
    total = own_ref[...] + got_ref[...].astype(F32)
    keep_ref[...] = total[:, :n]
    for j, ref in enumerate(send_refs):
        ref[...] = total[:, (j + 1) * n : (j + 2) * n].astype(BF16)


def curve_kernel(classes, keep_ref, *refs):
    got_refs, p_ref, c_ref = refs[:-2], refs[-2], refs[-1]
    total = keep_ref[...]
    for ref in got_refs:
        total = total + ref[...].astype(F32)
    total = total[:classes, :]
    prob = p_ref[...].astype(F32)
    mixed = jnp.sum(prob * total, axis=0, keepdims=True)
    c_ref[:classes, :] = (prob * (total - mixed)).astype(BF16)
    c_ref[classes:, :] = jnp.zeros((c_ref.shape[0] - classes, c_ref.shape[1]), BF16)


def share_kernel(count, skip, block, halves, *refs):
    left_refs, f_refs, o_ref = refs[:count], refs[count:-1], refs[-1]
    each = len(f_refs) // halves
    f = f_refs[0].shape[1]
    for h in range(halves):
        f_blocks = [(ref, at) for ref in f_refs[h * each : (h + 1) * each] for at in range(0, ref.shape[0], block)]
        total = None
        for left_ref, (f_ref, at) in zip(left_refs, f_blocks, strict=True):
            part = jnp.dot(left_ref[skip:, :], f_ref[at : at + block, :], preferred_element_type=F32)
            total = part if total is None else total + part
        o_ref[:, h * f : (h + 1) * f] = total.astype(o_ref.dtype)


def make_share(lefts, skip, feats, dtype):
    block = lefts[0].shape[1]
    wide, n, f = lefts[0].shape[0] - skip, block * len(lefts), sum(h[0].shape[1] for h in feats)
    return whole(
        functools.partial(share_kernel, len(lefts), skip, block, len(feats)),
        jax.ShapeDtypeStruct((wide, f), dtype),
        *lefts, *[a for h in feats for a in h], flops=2 * n * f * wide,
    )


def whole(kernel, shapes, *args, flops=0):
    size = sum(math.prod(a.shape) * a.dtype.itemsize for a in args)
    cost = pl.CostEstimate(flops=flops, bytes_accessed=size, transcendentals=0)
    return pl.pallas_call(kernel, out_shape=shapes, compiler_params=params(), cost_estimate=cost)(*args)


def on_device(line, ys, xs, inputs, probs, labels, proj_weight, phase, direction, damping):
    raw, own = inputs.shape
    classes = probs.shape[0]
    width = proj_weight.shape[1]
    depth = up(raw + 1, 16)
    wide = up(classes, 8)

    def swap_core(a):
        return lax.ppermute(a, "feat", [(i, i ^ 1) for i in range(2 * xs * ys)])

    def along(a, k):
        return lax.ppermute(a, "samp", [(i, (i + k) % line) for i in range(line)])

    def across(a, dy, dx):
        def to(i):
            y, x, c = i // (2 * xs), i // 2 % xs, i % 2
            return ((y + dy) % ys * xs + (x + dx) % xs) * 2 + c

        return lax.ppermute(a, "feat", [(i, to(i)) for i in range(2 * xs * ys)])

    offsets = [(dy, dx) for dy in range(ys) for dx in range(xs)]
    rows, half = depth + wide, width // 2
    (w_own,) = pack(
        functools.partial(pack_weights_kernel, raw, depth, classes),
        [jax.ShapeDtypeStruct((rows, width), BF16)],
        proj_weight, phase, direction,
    )
    ws = {(0, dx): across(w_own, 0, dx) for dx in range(1, xs)}
    ws.update({(dy, 0): across(w_own, dy, 0) for dy in range(1, ys)})
    far = [(dy, dx) for dy in range(1, ys) for dx in range(1, xs)]
    halves = {}
    for dy, dx in far:
        halves[dy, dx] = [across(ws[0, dx][:, :half], dy, 0), across(ws[dy, 0][:, half:], 0, dx)]
    x_own = pack(
        functools.partial(pack_samples_kernel, raw, depth, classes),
        jax.ShapeDtypeStruct((rows, own), BF16),
        inputs, probs, labels[None, :],
    )
    x_line = [x_own] + [along(x_own, k) for k in range(1, line)]

    feats = {at: [[]] for at in offsets}
    xts, totals = [], []

    def first(some):
        n = own * len(some)
        xt, total, *part = whole(
            functools.partial(first_kernel, depth, len(some), 1),
            [jax.ShapeDtypeStruct((n, depth), BF16), jax.ShapeDtypeStruct((n, wide), F32)]
            + [jax.ShapeDtypeStruct((n, width), BF16)],
            *some, w_own, flops=2 * n * width * (depth + wide),
        )
        xts.append(xt)
        totals.append(total)
        feats[0, 0][0] += part

    for k in range(line):
        first(x_line[k : k + 1])
        if k + 1 < line:
            x_line[k + 1], totals[k] = lax.optimization_barrier((x_line[k + 1], totals[k]))
    x_peer = [swap_core(a) for a in x_line]
    first(x_peer)
    blocks = x_line + x_peer
    near = list(ws)
    for group in (near, far):
        if group:
            last = group is far or not far
            pieces = [ws[at] for at in near] if group is near else [w for at in far for w in halves[at]]
            got, rest = make_next(xts, totals, pieces, depth, wide, own, last)
            for j, at in enumerate(group):
                feats[at] = [[got[j]]] if group is near else [[got[2 * j]], [got[2 * j + 1]]]
            totals = rest
    t_own, t_other = rest
    t_got = swap_core(t_other)
    lefts = blocks
    keep, *send = whole(
        spread_kernel,
        [jax.ShapeDtypeStruct((wide, own), F32)] + [jax.ShapeDtypeStruct((wide, own), BF16)] * (line - 1),
        t_own, t_got,
    )
    got = [along(a, -k) for k, a in enumerate(send, 1)]

    def collect(parts):
        out = parts[0, 0]
        for dy, dx in offsets[1:]:
            out = out + parts[dy, dx].astype(F32)
        return out[:classes]

    def send_home(lefts, skip):
        parts = {at: make_share(lefts, skip, feats[at], F32 if at == (0, 0) else BF16) for at in offsets[::-1]}
        return parts, {(dy, dx): across(parts[dy, dx], -dy, -dx) for dy, dx in offsets[1:]}

    parts, arrived = send_home(lefts, depth)
    keep, parts = lax.optimization_barrier((keep, parts))
    curv = whole(
        functools.partial(curve_kernel, classes), jax.ShapeDtypeStruct((wide, own), BF16), keep, *got, probs
    )
    c_line = [curv] + [along(curv, k) for k in range(1, line)]
    c_line, arrived = lax.optimization_barrier((c_line, arrived))
    curvs = c_line + [swap_core(a) for a in c_line]
    gradient = collect({(0, 0): parts[0, 0], **arrived})
    parts, arrived = send_home(curvs, 0)
    hess_vec = collect({(0, 0): parts[0, 0], **arrived}) + damping[0] * direction.astype(F32)
    return (hess_vec, gradient)


def solution(mesh):
    line, feat = mesh.shape["samp"], mesh.shape["feat"]
    ys = 2 if feat % 4 == 0 else 1
    xs = feat // (2 * ys)
    placed = (
        P(None, ("samp", "feat")),
        P(None, ("samp", "feat")),
        P(("samp", "feat")),
        P(None, ("feat", "samp")),
        P(None, ("feat", "samp")),
        P(None, ("feat", "samp")),
        P(),
    )
    return jax.shard_map(
        functools.partial(on_device, line, ys, xs),
        mesh=mesh,
        in_specs=placed,
        out_specs=(P(None, ("feat", "samp")), P(None, ("feat", "samp"))),
        check_vma=False,
    )
```

```python
import functools
import math

import jax
import jax.numpy as jnp
from jax import lax
from jax.experimental import pallas as pl
from jax.experimental.pallas import tpu as pltpu
from jax.sharding import PartitionSpec as P

F32, BF16 = jnp.float32, jnp.bfloat16
VMEM = 16 * 2**20
COEFS = (0.99995902, -19.73094237, 64.67144178, -82.39080631, 45.6210511)
ROUNDER = 12582912.0


def up(value, step):
    return -(-value // step) * step


def params():
    return pltpu.CompilerParams(vmem_limit_bytes=VMEM)


def cosine(angle):
    turns = angle * (0.5 / math.pi)
    rest = turns - jnp.round(turns)
    square = rest * rest
    total = square * COEFS[-1] + COEFS[-2]
    for coef in COEFS[-3::-1]:
        total = total * square + coef
    return total


def fetch(refs, bufs, sems):
    copies = [pltpu.make_async_copy(ref, buf, sems.at[j]) for j, (ref, buf) in enumerate(zip(refs, bufs, strict=True))]
    for copy in copies:
        copy.start()
    for copy in copies:
        copy.wait()


def pack_weights_kernel(raw, depth, classes, w_hbm, ph_hbm, d_hbm, *refs):
    o_refs, (w_ref, ph_ref, d_ref, sems) = refs[:-4], refs[-4:]
    fetch((w_hbm, ph_hbm, d_hbm), (w_ref, ph_ref, d_ref), sems)
    rows, f = o_refs[0].shape
    for j, o_ref in enumerate(o_refs):
        here = slice(j * f, (j + 1) * f)
        o_ref[:raw, :] = w_ref[:, here]
        head = lax.broadcasted_iota(jnp.int32, (depth - raw, f), 0) == 0
        o_ref[raw:depth, :] = jnp.where(head, ph_ref[:, here].astype(F32), 0.0).astype(BF16)
        o_ref[depth : depth + classes, :] = d_ref[:, here]
        o_ref[depth + classes :, :] = jnp.zeros((rows - depth - classes, f), BF16)


def pack_samples_kernel(raw, depth, classes, x_hbm, p_hbm, l_hbm, o_ref, x_ref, p_ref, l_ref, sems):
    fetch((x_hbm, p_hbm, l_hbm), (x_ref, p_ref, l_ref), sems)
    rows, n = o_ref.shape
    o_ref[:raw, :] = x_ref[...]
    head = lax.broadcasted_iota(jnp.int32, (depth - raw, n), 0) == 0
    o_ref[raw:depth, :] = jnp.where(head, 1.0, 0.0).astype(BF16)
    ids = lax.broadcasted_iota(jnp.int32, (classes, n), 0)
    onehot = (ids == l_ref[...]).astype(F32)
    o_ref[depth : depth + classes, :] = (p_ref[...].astype(F32) - onehot).astype(BF16)
    o_ref[depth + classes :, :] = jnp.zeros((rows - depth - classes, n), BF16)


def pack(kernel, shapes, *args):
    return pl.pallas_call(
        kernel,
        in_specs=[pl.BlockSpec(memory_space=pltpu.HBM)] * len(args),
        out_shape=shapes,
        scratch_shapes=[pltpu.VMEM(a.shape, a.dtype) for a in args] + [pltpu.SemaphoreType.DMA((len(args),))],
        compiler_params=params(),
    )(*args)


def one_block(xt, w_ref, depth):
    feats = cosine(jnp.dot(xt, w_ref[:depth, :], preferred_element_type=F32)).astype(BF16)
    dims = (((1,), (1,)), ((), ()))
    return feats, lax.dot_general(feats, w_ref[depth:, :], dims, preferred_element_type=F32)


def first_kernel(depth, count, parts, *refs):
    x_refs, w_refs = refs[:count], refs[count : count + parts]
    xt_ref, t_ref, *f_refs = refs[count + parts :]
    n = x_refs[0].shape[1]
    for j in range(count):
        here = slice(j * n, (j + 1) * n)
        xt = x_refs[j][:depth, :].T
        xt_ref[here, :] = xt
        total = None
        for w_ref, f_ref in zip(w_refs, f_refs, strict=True):
            f_ref[here, :], tangent = one_block(xt, w_ref, depth)
            total = tangent if total is None else total + tangent
        t_ref[here, :] = total


def next_kernel(depth, count, totals, parts, block, last, *refs):
    xt_refs, t_refs = refs[:count], refs[count : count + totals]
    refs = refs[count + totals :]
    w_refs, f_refs, out_refs = refs[:parts], refs[parts : 2 * parts], refs[2 * parts :]
    t_blocks = [(ref, at) for ref in t_refs for at in range(0, ref.shape[0], block)]
    spot = 0
    for xt_ref in xt_refs:
        for at in range(0, xt_ref.shape[0], block):
            t_ref, t_at = t_blocks[spot // block]
            xt, total = xt_ref[at : at + block, :], t_ref[t_at : t_at + block, :]
            for w_ref, f_ref in zip(w_refs, f_refs, strict=True):
                f_ref[spot : spot + block, :], tangent = one_block(xt, w_ref, depth)
                total = total + tangent
            if not last:
                here = spot % out_refs[0].shape[0]
                out_refs[spot // out_refs[0].shape[0]][here : here + block, :] = total
            else:
                out_refs[0][:, spot : spot + block] = total.T.astype(out_refs[0].dtype)
            spot += block


def make_next(xts, totals, pieces, depth, wide, block, last=None):
    n, f = sum(a.shape[0] for a in xts), pieces[0].shape[1]
    shapes = [jax.ShapeDtypeStruct((n, f), BF16)] * len(pieces)
    if last is None:
        shapes += [jax.ShapeDtypeStruct((n // 2, wide), F32)] * 2
    else:
        shapes.append(jax.ShapeDtypeStruct((wide, n), last))
    kernel = functools.partial(next_kernel, depth, len(xts), len(totals), len(pieces), block, last is not None)
    out = whole(kernel, shapes, *xts, *totals, *pieces, flops=2 * n * f * len(pieces) * (depth + wide))
    return out[: len(pieces)], out[len(pieces) :]


def spread_kernel(own_ref, got_ref, keep_ref, *send_refs):
    n = keep_ref.shape[1]
    total = own_ref[...] + got_ref[...].astype(F32)
    keep_ref[...] = total[:, :n]
    for j, ref in enumerate(send_refs):
        ref[...] = total[:, (j + 1) * n : (j + 2) * n].astype(BF16)


def curve_kernel(classes, keep_ref, *refs):
    got_refs, p_ref, c_ref = refs[:-2], refs[-2], refs[-1]
    total = keep_ref[...]
    for ref in got_refs:
        total = total + ref[...].astype(F32)
    total = total[:classes, :]
    prob = p_ref[...].astype(F32)
    mixed = jnp.sum(prob * total, axis=0, keepdims=True)
    c_ref[:classes, :] = (prob * (total - mixed)).astype(BF16)
    c_ref[classes:, :] = jnp.zeros((c_ref.shape[0] - classes, c_ref.shape[1]), BF16)


def share_kernel(count, skip, block, halves, outs, *refs):
    left_refs, f_refs, o_refs = refs[:count], refs[count:-outs], refs[-outs:]
    each = len(f_refs) // halves
    f = f_refs[0].shape[1]
    for h in range(halves):
        f_blocks = [(ref, at) for ref in f_refs[h * each : (h + 1) * each] for at in range(0, ref.shape[0], block)]
        total = None
        for left_ref, (f_ref, at) in zip(left_refs, f_blocks, strict=True):
            part = jnp.dot(left_ref[skip:, :], f_ref[at : at + block, :], preferred_element_type=F32)
            total = part if total is None else total + part
        if outs == 1:
            o_refs[0][:, h * f : (h + 1) * f] = total.astype(o_refs[0].dtype)
        else:
            o_refs[h][...] = total.astype(o_refs[h].dtype)


def add_kernel(side, own_ref, *refs):
    add_refs, o_ref = refs[:-1], refs[-1]
    half = own_ref.shape[1] // 2
    for h in (0, 1):
        here = slice(h * half, (h + 1) * half)
        total = own_ref[:, here]
        for ref in add_refs if h == side else ():
            total = total + ref[...].astype(F32)
        o_ref[:, here] = total.astype(o_ref.dtype)


def make_share(lefts, skip, feats, dtype, apart=False):
    block = lefts[0].shape[1]
    wide, n, f = lefts[0].shape[0] - skip, block * len(lefts), sum(h[0].shape[1] for h in feats)
    return whole(
        functools.partial(share_kernel, len(lefts), skip, block, len(feats), len(feats) if apart else 1),
        [jax.ShapeDtypeStruct((wide, f // 2), dtype)] * 2 if apart else jax.ShapeDtypeStruct((wide, f), dtype),
        *lefts, *[a for h in feats for a in h], flops=2 * n * f * wide,
    )


def whole(kernel, shapes, *args, flops=0):
    size = sum(math.prod(a.shape) * a.dtype.itemsize for a in args)
    cost = pl.CostEstimate(flops=flops, bytes_accessed=size, transcendentals=0)
    return pl.pallas_call(kernel, out_shape=shapes, compiler_params=params(), cost_estimate=cost)(*args)


def on_device(line, ys, xs, inputs, probs, labels, proj_weight, phase, direction, damping):
    raw, own = inputs.shape
    classes = probs.shape[0]
    width = proj_weight.shape[1]
    depth = up(raw + 1, 16)
    wide = up(classes, 8)

    def swap_core(a):
        return lax.ppermute(a, "feat", [(i, i ^ 1) for i in range(2 * xs * ys)])

    def along(a, k):
        def to(i):
            return i ^ abs(k) if line & (line - 1) == 0 else (i + k) % line

        return lax.ppermute(a, "samp", [(i, to(i)) for i in range(line)])

    places = (1, 2, 3) if line == 4 else range(1, line)

    def across(a, dy, dx):
        def to(i):
            y, x, c = i // (2 * xs), i // 2 % xs, i % 2
            return ((y + dy) % ys * xs + (x + dx) % xs) * 2 + c

        return lax.ppermute(a, "feat", [(i, to(i)) for i in range(2 * xs * ys)])

    offsets = [(dy, dx) for dy in range(ys) for dx in range(xs)]
    rows, half = depth + wide, width // 2
    (w_own,) = pack(
        functools.partial(pack_weights_kernel, raw, depth, classes),
        [jax.ShapeDtypeStruct((rows, width), BF16)],
        proj_weight, phase, direction,
    )
    ws = {(0, dx): across(w_own, 0, dx) for dx in range(1, xs)}
    ws.update({(dy, 0): across(w_own, dy, 0) for dy in range(1, ys)})
    far = [(dy, dx) for dy in range(1, ys) for dx in range(1, xs)]
    halves = {}
    for dy, dx in far:
        halves[dy, dx] = [across(ws[0, dx][:, :half], dy, 0), across(ws[dy, 0][:, half:], 0, dx)]
    x_own = pack(
        functools.partial(pack_samples_kernel, raw, depth, classes),
        jax.ShapeDtypeStruct((rows, own), BF16),
        inputs, probs, labels[None, :],
    )
    x_line = [x_own] + [along(x_own, k) for k in places]

    feats = {at: [[]] for at in offsets}
    xts, totals = [], []

    def first(some):
        n = own * len(some)
        xt, total, *part = whole(
            functools.partial(first_kernel, depth, len(some), 1),
            [jax.ShapeDtypeStruct((n, depth), BF16), jax.ShapeDtypeStruct((n, wide), F32)]
            + [jax.ShapeDtypeStruct((n, width), BF16)],
            *some, w_own, flops=2 * n * width * (depth + wide),
        )
        xts.append(xt)
        totals.append(total)
        feats[0, 0][0] += part

    for k in range(line):
        first(x_line[k : k + 1])
        if k + 1 < line:
            x_line[k + 1], totals[k] = lax.optimization_barrier((x_line[k + 1], totals[k]))
    x_peer = [swap_core(a) for a in x_line]
    first(x_peer)
    blocks = x_line + x_peer
    near = list(ws)
    got, totals = make_next(xts, totals, [ws[at] for at in near], depth, wide, own)
    for at, piece in zip(near, got, strict=True):
        feats[at] = [[piece]]

    def share(at, lefts, skip):
        return make_share(lefts, skip, feats[at], F32 if at == (0, 0) else BF16)

    def home(at, part):
        return across(part, -at[0], -at[1])

    parts = {at: share(at, blocks, depth) for at in near}
    totals, parts = lax.optimization_barrier((totals, parts))
    arrived = {at: home(at, parts[at]) for at in near}
    turned = []
    pieces = [w for at in far for w in halves[at]]
    for some, total, dtype in ((xts[-1:], totals[1], BF16), (xts[:-1], totals[0], F32)):
        got, (out,) = make_next(some, [total], pieces, depth, wide, own, dtype)
        turned.append((got, out))
    for j, at in enumerate(far):
        feats[at] = [[turned[1][0][2 * j + h], turned[0][0][2 * j + h]] for h in (0, 1)]
    t_other, t_own = turned[0][1], turned[1][1]
    t_got = swap_core(t_other)
    keep, *send = whole(
        spread_kernel,
        [jax.ShapeDtypeStruct((wide, own), F32)] + [jax.ShapeDtypeStruct((wide, own), BF16)] * (line - 1),
        t_own, t_got,
    )
    got = [along(a, -k) for k, a in zip(places, send, strict=True)]

    def collect(parts, some):
        out = parts[0, 0]
        for dy, dx in some:
            out = out + parts[dy, dx].astype(F32)
        return out[:classes]

    parts.update({at: share(at, blocks, depth) for at in far + [(0, 0)]})
    arrived.update({at: home(at, parts[at]) for at in far})
    keep, parts = lax.optimization_barrier((keep, parts))
    curv = whole(
        functools.partial(curve_kernel, classes), jax.ShapeDtypeStruct((wide, own), BF16), keep, *got, probs
    )
    c_line = [curv] + [along(curv, k) for k in places]
    c_line, arrived = lax.optimization_barrier((c_line, arrived))
    curvs = c_line + [swap_core(a) for a in c_line]
    gradient = collect({(0, 0): parts[0, 0], **arrived}, offsets[1:])
    thirds = {at: make_share(curvs, 0, feats[at], BF16, apart=True) for at in far}
    curvs, thirds = lax.optimization_barrier((curvs, thirds))
    first_half = {(dy, dx): across(thirds[dy, dx][0], 0, -dx) for dy, dx in far}
    second_half = {(dy, dx): across(thirds[dy, dx][1], -dy, 0) for dy, dx in far}
    parts, arrived = {}, {}
    for at in near:
        plain = make_share(curvs, 0, feats[at], F32)
        others = [first_half[f] if at[0] else second_half[f] for f in far if at[0] in (0, f[0]) and at[1] in (0, f[1])]
        h = 0 if at[0] else 1
        parts[at] = whole(functools.partial(add_kernel, h), jax.ShapeDtypeStruct(plain.shape, BF16), plain, *others)
        arrived[at] = home(at, parts[at])
    parts[0, 0] = share((0, 0), curvs, 0)
    hess_vec = collect({(0, 0): parts[0, 0], **arrived}, near) + damping[0] * direction.astype(F32)
    return (hess_vec, gradient)


def solution(mesh):
    line, feat = mesh.shape["samp"], mesh.shape["feat"]
    ys = 2 if feat % 4 == 0 else 1
    xs = feat // (2 * ys)
    placed = (
        P(None, ("samp", "feat")),
        P(None, ("samp", "feat")),
        P(("samp", "feat")),
        P(None, ("feat", "samp")),
        P(None, ("feat", "samp")),
        P(None, ("feat", "samp")),
        P(),
    )
    return jax.shard_map(
        functools.partial(on_device, line, ys, xs),
        mesh=mesh,
        in_specs=placed,
        out_specs=(P(None, ("feat", "samp")), P(None, ("feat", "samp"))),
        check_vma=False,
    )
```

```python
import functools
import math

import jax
import jax.numpy as jnp
from jax import lax
from jax.experimental import pallas as pl
from jax.experimental.pallas import tpu as pltpu
from jax.sharding import PartitionSpec as P

F32, BF16 = jnp.float32, jnp.bfloat16
VMEM = 16 * 2**20
COEFS = (0.99995902, -19.73094237, 64.67144178, -82.39080631, 45.6210511)
ROUNDER = 12582912.0


def up(value, step):
    return -(-value // step) * step


def params():
    return pltpu.CompilerParams(vmem_limit_bytes=VMEM)


def cosine(angle):
    turns = angle * (0.5 / math.pi)
    rest = turns - jnp.round(turns)
    square = rest * rest
    total = square * COEFS[-1] + COEFS[-2]
    for coef in COEFS[-3::-1]:
        total = total * square + coef
    return total


def fetch(refs, bufs, sems):
    copies = [pltpu.make_async_copy(ref, buf, sems.at[j]) for j, (ref, buf) in enumerate(zip(refs, bufs, strict=True))]
    for copy in copies:
        copy.start()
    for copy in copies:
        copy.wait()


def pack_weights_kernel(raw, depth, classes, w_hbm, ph_hbm, d_hbm, *refs):
    o_refs, (w_ref, ph_ref, d_ref, sems) = refs[:-4], refs[-4:]
    fetch((w_hbm, ph_hbm, d_hbm), (w_ref, ph_ref, d_ref), sems)
    rows, f = o_refs[0].shape
    for j, o_ref in enumerate(o_refs):
        here = slice(j * f, (j + 1) * f)
        o_ref[:raw, :] = w_ref[:, here]
        head = lax.broadcasted_iota(jnp.int32, (depth - raw, f), 0) == 0
        o_ref[raw:depth, :] = jnp.where(head, ph_ref[:, here].astype(F32), 0.0).astype(BF16)
        o_ref[depth : depth + classes, :] = d_ref[:, here]
        o_ref[depth + classes :, :] = jnp.zeros((rows - depth - classes, f), BF16)


def pack_samples_kernel(raw, depth, classes, x_hbm, p_hbm, l_hbm, o_ref, x_ref, p_ref, l_ref, sems):
    fetch((x_hbm, p_hbm, l_hbm), (x_ref, p_ref, l_ref), sems)
    rows, n = o_ref.shape
    o_ref[:raw, :] = x_ref[...]
    head = lax.broadcasted_iota(jnp.int32, (depth - raw, n), 0) == 0
    o_ref[raw:depth, :] = jnp.where(head, 1.0, 0.0).astype(BF16)
    ids = lax.broadcasted_iota(jnp.int32, (classes, n), 0)
    onehot = (ids == l_ref[...]).astype(F32)
    o_ref[depth : depth + classes, :] = (p_ref[...].astype(F32) - onehot).astype(BF16)
    o_ref[depth + classes :, :] = jnp.zeros((rows - depth - classes, n), BF16)


def pack(kernel, shapes, *args):
    return pl.pallas_call(
        kernel,
        in_specs=[pl.BlockSpec(memory_space=pltpu.HBM)] * len(args),
        out_shape=shapes,
        scratch_shapes=[pltpu.VMEM(a.shape, a.dtype) for a in args] + [pltpu.SemaphoreType.DMA((len(args),))],
        compiler_params=params(),
    )(*args)


def one_block(xt, w_ref, depth):
    feats = cosine(jnp.dot(xt, w_ref[:depth, :], preferred_element_type=F32)).astype(BF16)
    dims = (((1,), (1,)), ((), ()))
    return feats, lax.dot_general(feats, w_ref[depth:, :], dims, preferred_element_type=F32)


def first_kernel(depth, count, parts, *refs):
    x_refs, w_refs = refs[:count], refs[count : count + parts]
    xt_ref, t_ref, *f_refs = refs[count + parts :]
    n = x_refs[0].shape[1]
    for j in range(count):
        here = slice(j * n, (j + 1) * n)
        xt = x_refs[j][:depth, :].T
        xt_ref[here, :] = xt
        total = None
        for w_ref, f_ref in zip(w_refs, f_refs, strict=True):
            f_ref[here, :], tangent = one_block(xt, w_ref, depth)
            total = tangent if total is None else total + tangent
        t_ref[here, :] = total


def next_kernel(depth, count, totals, parts, block, last, *refs):
    xt_refs, t_refs = refs[:count], refs[count : count + totals]
    refs = refs[count + totals :]
    w_refs, f_refs, out_refs = refs[:parts], refs[parts : 2 * parts], refs[2 * parts :]
    t_blocks = [(ref, at) for ref in t_refs for at in range(0, ref.shape[0], block)]
    spot = 0
    for xt_ref in xt_refs:
        for at in range(0, xt_ref.shape[0], block):
            t_ref, t_at = t_blocks[spot // block]
            xt, total = xt_ref[at : at + block, :], t_ref[t_at : t_at + block, :]
            for w_ref, f_ref in zip(w_refs, f_refs, strict=True):
                f_ref[spot : spot + block, :], tangent = one_block(xt, w_ref, depth)
                total = total + tangent
            if not last:
                here = spot % out_refs[0].shape[0]
                out_refs[spot // out_refs[0].shape[0]][here : here + block, :] = total
            else:
                out_refs[0][:, spot : spot + block] = total.T.astype(out_refs[0].dtype)
            spot += block


def make_next(xts, totals, pieces, depth, wide, block, last=None):
    n, f = sum(a.shape[0] for a in xts), pieces[0].shape[1]
    shapes = [jax.ShapeDtypeStruct((n, f), BF16)] * len(pieces)
    if last is None:
        shapes += [jax.ShapeDtypeStruct((n // 2, wide), F32)] * 2
    else:
        shapes.append(jax.ShapeDtypeStruct((wide, n), last))
    kernel = functools.partial(next_kernel, depth, len(xts), len(totals), len(pieces), block, last is not None)
    out = whole(kernel, shapes, *xts, *totals, *pieces, flops=2 * n * f * len(pieces) * (depth + wide))
    return out[: len(pieces)], out[len(pieces) :]


def spread_kernel(own_ref, got_ref, keep_ref, *send_refs):
    n = keep_ref.shape[1]
    total = own_ref[...] + got_ref[...].astype(F32)
    keep_ref[...] = total[:, :n]
    for j, ref in enumerate(send_refs):
        ref[...] = total[:, (j + 1) * n : (j + 2) * n].astype(BF16)


def curve_kernel(classes, keep_ref, *refs):
    got_refs, p_ref, c_ref = refs[:-2], refs[-2], refs[-1]
    total = keep_ref[...]
    for ref in got_refs:
        total = total + ref[...].astype(F32)
    total = total[:classes, :]
    prob = p_ref[...].astype(F32)
    mixed = jnp.sum(prob * total, axis=0, keepdims=True)
    c_ref[:classes, :] = (prob * (total - mixed)).astype(BF16)
    c_ref[classes:, :] = jnp.zeros((c_ref.shape[0] - classes, c_ref.shape[1]), BF16)


def share_kernel(count, start, skip, block, halves, outs, seeded, *refs):
    left_refs, f_refs, o_refs = refs[:count], refs[count:-outs], refs[-outs:]
    seed_ref, f_refs = (f_refs[0], f_refs[1:]) if seeded else (None, f_refs)
    each = len(f_refs) // halves
    f = f_refs[0].shape[1]
    for h in range(halves):
        f_blocks = [(ref, at) for ref in f_refs[h * each : (h + 1) * each] for at in range(0, ref.shape[0], block)]
        total = seed_ref[:, h * f : (h + 1) * f] if seeded else None
        for left_ref, (f_ref, at) in zip(left_refs, f_blocks[start : start + count], strict=True):
            part = jnp.dot(left_ref[skip:, :], f_ref[at : at + block, :], preferred_element_type=F32)
            total = part if total is None else total + part
        if outs == 1:
            o_refs[0][:, h * f : (h + 1) * f] = total.astype(o_refs[0].dtype)
        else:
            for j in range(outs // halves):
                wide = f * halves // outs
                o_refs[h * (outs // halves) + j][...] = total[:, j * wide : (j + 1) * wide].astype(o_refs[0].dtype)


def add_kernel(*refs):
    total = refs[0][...].astype(F32)
    for ref in refs[1:-1]:
        total = total + ref[...].astype(F32)
    refs[-1][...] = total.astype(refs[-1].dtype)


def make_share(lefts, skip, feats, dtype, start=0, seed=None, outs=1):
    block = lefts[0].shape[1]
    wide, n, f = lefts[0].shape[0] - skip, block * len(lefts), sum(h[0].shape[1] for h in feats)
    shapes = [jax.ShapeDtypeStruct((wide, f // outs), dtype)] * outs
    return whole(
        functools.partial(share_kernel, len(lefts), start, skip, block, len(feats), outs, seed is not None),
        shapes if outs > 1 else shapes[0],
        *lefts, *([] if seed is None else [seed]), *[a for h in feats for a in h], flops=2 * n * f * wide,
    )


def whole(kernel, shapes, *args, flops=0, weight=1):
    size = sum(math.prod(a.shape) * a.dtype.itemsize for a in args)
    cost = pl.CostEstimate(flops=weight * flops, bytes_accessed=weight * size, transcendentals=0)
    return pl.pallas_call(kernel, out_shape=shapes, compiler_params=params(), cost_estimate=cost)(*args)


def on_device(line, ys, xs, inputs, probs, labels, proj_weight, phase, direction, damping):
    raw, own = inputs.shape
    classes = probs.shape[0]
    width = proj_weight.shape[1]
    depth = up(raw + 1, 16)
    wide = up(classes, 8)

    def swap_core(a):
        return lax.ppermute(a, "feat", [(i, i ^ 1) for i in range(2 * xs * ys)])

    def along(a, k):
        def to(i):
            return i ^ abs(k) if line & (line - 1) == 0 else (i + k) % line

        return lax.ppermute(a, "samp", [(i, to(i)) for i in range(line)])

    places = (1, 2, 3) if line == 4 else range(1, line)

    def across(a, dy, dx):
        def to(i):
            y, x, c = i // (2 * xs), i // 2 % xs, i % 2
            return ((y + dy) % ys * xs + (x + dx) % xs) * 2 + c

        return lax.ppermute(a, "feat", [(i, to(i)) for i in range(2 * xs * ys)])

    offsets = [(dy, dx) for dy in range(ys) for dx in range(xs)]
    rows, half = depth + wide, width // 2
    w_own = jnp.concatenate(
        [
            proj_weight,
            jnp.pad(phase, ((0, depth - raw - 1), (0, 0))),
            jnp.pad(direction, ((0, wide - classes), (0, 0))),
        ]
    )
    ws = {(0, dx): across(w_own, 0, dx) for dx in range(1, xs)}
    ws.update({(dy, 0): across(w_own, dy, 0) for dy in range(1, ys)})
    far = [(dy, dx) for dy in range(1, ys) for dx in range(1, xs)]
    halves = {}
    for dy, dx in far:
        halves[dy, dx] = [across(ws[0, dx][:, :half], dy, 0), across(ws[dy, 0][:, half:], 0, dx)]
    onehot = lax.broadcasted_iota(jnp.int32, probs.shape, 0) == labels[None, :]
    resid = (probs.astype(F32) - onehot.astype(F32)).astype(BF16)
    x_own = jnp.concatenate(
        [
            inputs,
            jnp.ones((1, own), BF16),
            jnp.zeros((depth - raw - 1, own), BF16),
            jnp.pad(resid, ((0, wide - classes), (0, 0))),
        ]
    )
    x_line = [x_own] + [along(x_own, k) for k in places]

    feats = {at: [[]] for at in offsets}
    xts, totals = [], []

    def first(some):
        n = own * len(some)
        xt, total, *part = whole(
            functools.partial(first_kernel, depth, len(some), 1),
            [jax.ShapeDtypeStruct((n, depth), BF16), jax.ShapeDtypeStruct((n, wide), F32)]
            + [jax.ShapeDtypeStruct((n, width), BF16)],
            *some, w_own, flops=2 * n * width * (depth + wide),
        )
        xts.append(xt)
        totals.append(total)
        feats[0, 0][0] += part

    for k in range(line):
        first(x_line[k : k + 1])
        if k + 1 < line:
            x_line[k + 1], totals[k] = lax.optimization_barrier((x_line[k + 1], totals[k]))
    x_peer = [swap_core(a) for a in x_line]
    first(x_peer)
    blocks = x_line + x_peer
    near = list(ws)
    got, totals = make_next(xts, totals, [ws[at] for at in near], depth, wide, own)
    for at, piece in zip(near, got, strict=True):
        feats[at] = [[piece]]

    def share(at, lefts, skip):
        return make_share(lefts, skip, feats[at], F32 if at == (0, 0) else BF16)

    def home(at, part):
        return across(part, -at[0], -at[1])

    parts = {at: share(at, blocks, depth) for at in near}
    totals, parts = lax.optimization_barrier((totals, parts))
    arrived = {at: home(at, parts[at]) for at in near}
    turned = []
    pieces = [w for at in far for w in halves[at]]
    for some, total, dtype in ((xts[-1:], totals[1], BF16), (xts[:-1], totals[0], F32)):
        got, (out,) = make_next(some, [total], pieces, depth, wide, own, dtype)
        turned.append((got, out))
    for j, at in enumerate(far):
        feats[at] = [[turned[1][0][2 * j + h], turned[0][0][2 * j + h]] for h in (0, 1)]
    t_other, t_own = turned[0][1], turned[1][1]
    t_got = swap_core(t_other)
    keep, *send = whole(
        spread_kernel,
        [jax.ShapeDtypeStruct((wide, own), F32)] + [jax.ShapeDtypeStruct((wide, own), BF16)] * (line - 1),
        t_own, t_got,
    )
    got = [along(a, -k) for k, a in zip(places, send, strict=True)]

    def collect(parts, some):
        out = parts[0, 0]
        for dy, dx in some:
            out = out + parts[dy, dx].astype(F32)
        return out[:classes]

    parts[0, 0] = share((0, 0), blocks, depth)
    keep, parts = lax.optimization_barrier((keep, parts))
    got, after = lax.optimization_barrier((got, blocks))
    parts.update({at: share(at, after, depth) for at in far})
    arrived.update({at: home(at, parts[at]) for at in far})
    curv = whole(
        functools.partial(curve_kernel, classes), jax.ShapeDtypeStruct((wide, own), BF16), keep, *got, probs
    )
    c_line = [curv] + [along(curv, k) for k in places]
    c_line, ready = lax.optimization_barrier((c_line, {at: arrived[at] for at in near}))
    c_peer = [swap_core(a) for a in c_line]
    seeds = {at: make_share(c_line, 0, feats[at], F32) for at in offsets[::-1]}

    def total_share(at, dtype, outs=1):
        return make_share(c_peer, 0, feats[at], dtype, line, seeds[at], outs)

    thirds = {at: total_share(at, BF16, 2) for at in far}
    c_peer, thirds = lax.optimization_barrier((c_peer, thirds))
    first_half = {(dy, dx): across(thirds[dy, dx][0], 0, -dx) for dy, dx in far}
    second_half = {(dy, dx): across(thirds[dy, dx][1], -dy, 0) for dy, dx in far}
    rest = {at: arrived[at] for at in far}
    first_half, second_half, rest = lax.optimization_barrier((first_half, second_half, rest))
    arrived = {**ready, **rest}
    gradient = collect({(0, 0): parts[0, 0], **arrived}, offsets[1:])
    hess = total_share((0, 0), F32)
    sides = [hess[:classes, :half], hess[:classes, half:]]
    for at in near:
        h = 0 if at[0] else 1
        plain = total_share(at, BF16, 2)
        others = [first_half[f] if at[0] else second_half[f] for f in far if at[0] in (0, f[0]) and at[1] in (0, f[1])]
        mixed = whole(add_kernel, jax.ShapeDtypeStruct(plain[h].shape, BF16), plain[h], *others)
        for side, piece in ((1 - h, home(at, plain[1 - h])), (h, home(at, mixed))):
            sides[side] = sides[side] + piece[:classes].astype(F32)
    hess_vec = jnp.concatenate(sides, axis=1) + damping[0] * direction.astype(F32)
    return (hess_vec, gradient)


def solution(mesh):
    line, feat = mesh.shape["samp"], mesh.shape["feat"]
    ys = 2 if feat % 4 == 0 else 1
    xs = feat // (2 * ys)
    placed = (
        P(None, ("samp", "feat")),
        P(None, ("samp", "feat")),
        P(("samp", "feat")),
        P(None, ("feat", "samp")),
        P(None, ("feat", "samp")),
        P(None, ("feat", "samp")),
        P(),
    )
    return jax.shard_map(
        functools.partial(on_device, line, ys, xs),
        mesh=mesh,
        in_specs=placed,
        out_specs=(P(None, ("feat", "samp")), P(None, ("feat", "samp"))),
        check_vma=False,
    )
```

```python
import functools
import math

import jax
import jax.numpy as jnp
from jax import lax
from jax.experimental import pallas as pl
from jax.experimental.pallas import tpu as pltpu
from jax.sharding import PartitionSpec as P

F32, BF16 = jnp.float32, jnp.bfloat16
VMEM = 16 * 2**20
COEFS = (0.99995902, -19.73094237, 64.67144178, -82.39080631, 45.6210511)
ROUNDER = 12582912.0


def up(value, step):
    return -(-value // step) * step


def params():
    return pltpu.CompilerParams(vmem_limit_bytes=VMEM)


def cosine(angle):
    turns = angle * (0.5 / math.pi)
    rest = turns - jnp.round(turns)
    square = rest * rest
    total = square * COEFS[-1] + COEFS[-2]
    for coef in COEFS[-3::-1]:
        total = total * square + coef
    return total


def fetch(refs, bufs, sems):
    copies = [pltpu.make_async_copy(ref, buf, sems.at[j]) for j, (ref, buf) in enumerate(zip(refs, bufs, strict=True))]
    for copy in copies:
        copy.start()
    for copy in copies:
        copy.wait()


def pack_weights_kernel(raw, depth, classes, w_hbm, ph_hbm, d_hbm, *refs):
    o_refs, (w_ref, ph_ref, d_ref, sems) = refs[:-4], refs[-4:]
    fetch((w_hbm, ph_hbm, d_hbm), (w_ref, ph_ref, d_ref), sems)
    rows, f = o_refs[0].shape
    for j, o_ref in enumerate(o_refs):
        here = slice(j * f, (j + 1) * f)
        o_ref[:raw, :] = w_ref[:, here]
        head = lax.broadcasted_iota(jnp.int32, (depth - raw, f), 0) == 0
        o_ref[raw:depth, :] = jnp.where(head, ph_ref[:, here].astype(F32), 0.0).astype(BF16)
        o_ref[depth : depth + classes, :] = d_ref[:, here]
        o_ref[depth + classes :, :] = jnp.zeros((rows - depth - classes, f), BF16)


def pack_samples_kernel(raw, depth, classes, x_hbm, p_hbm, l_hbm, o_ref, x_ref, p_ref, l_ref, sems):
    fetch((x_hbm, p_hbm, l_hbm), (x_ref, p_ref, l_ref), sems)
    rows, n = o_ref.shape
    o_ref[:raw, :] = x_ref[...]
    head = lax.broadcasted_iota(jnp.int32, (depth - raw, n), 0) == 0
    o_ref[raw:depth, :] = jnp.where(head, 1.0, 0.0).astype(BF16)
    ids = lax.broadcasted_iota(jnp.int32, (classes, n), 0)
    onehot = (ids == l_ref[...]).astype(F32)
    o_ref[depth : depth + classes, :] = (p_ref[...].astype(F32) - onehot).astype(BF16)
    o_ref[depth + classes :, :] = jnp.zeros((rows - depth - classes, n), BF16)


def pack(kernel, shapes, *args):
    return pl.pallas_call(
        kernel,
        in_specs=[pl.BlockSpec(memory_space=pltpu.HBM)] * len(args),
        out_shape=shapes,
        scratch_shapes=[pltpu.VMEM(a.shape, a.dtype) for a in args] + [pltpu.SemaphoreType.DMA((len(args),))],
        compiler_params=params(),
    )(*args)


def one_block(xt, w_ref, depth):
    feats = cosine(jnp.dot(xt, w_ref[:depth, :], preferred_element_type=F32)).astype(BF16)
    dims = (((1,), (1,)), ((), ()))
    return feats, lax.dot_general(feats, w_ref[depth:, :], dims, preferred_element_type=F32)


def first_kernel(depth, count, parts, *refs):
    x_refs, w_refs = refs[:count], refs[count : count + parts]
    xt_ref, t_ref, *f_refs = refs[count + parts :]
    n = x_refs[0].shape[1]
    for j in range(count):
        here = slice(j * n, (j + 1) * n)
        xt = x_refs[j][:depth, :].T
        xt_ref[here, :] = xt
        total = None
        for w_ref, f_ref in zip(w_refs, f_refs, strict=True):
            f_ref[here, :], tangent = one_block(xt, w_ref, depth)
            total = tangent if total is None else total + tangent
        t_ref[here, :] = total


def rows_of(refs, block, group):
    pieces = [(ref, at) for ref in refs for at in range(0, ref.shape[0], block)]
    return [pieces[j : j + group] for j in range(0, len(pieces), group)]


def load(pieces, block):
    (first, start), (_, end) = pieces[0], pieces[-1]
    if all(ref is first for ref, _ in pieces):
        return first[start : end + block, :]
    return jnp.concatenate([ref[at : at + block, :] for ref, at in pieces], axis=0)


def next_kernel(depth, count, totals, parts, block, last, *refs):
    xt_refs, t_refs = refs[:count], refs[count : count + totals]
    refs = refs[count + totals :]
    w_refs, f_refs, out_refs = refs[:parts], refs[parts : 2 * parts], refs[2 * parts :]
    spot = 0
    for xt_pieces, t_pieces in zip(rows_of(xt_refs, block, 2), rows_of(t_refs, block, 2), strict=True):
        xt, total = load(xt_pieces, block), load(t_pieces, block)
        n = xt.shape[0]
        for w_ref, f_ref in zip(w_refs, f_refs, strict=True):
            f_ref[spot : spot + n, :], tangent = one_block(xt, w_ref, depth)
            total = total + tangent
        if not last:
            here = spot % out_refs[0].shape[0]
            out_refs[spot // out_refs[0].shape[0]][here : here + n, :] = total
        else:
            out_refs[0][:, spot : spot + n] = total.T.astype(out_refs[0].dtype)
        spot += n


def make_next(xts, totals, pieces, depth, wide, block, last=None):
    n, f = sum(a.shape[0] for a in xts), pieces[0].shape[1]
    shapes = [jax.ShapeDtypeStruct((n, f), BF16)] * len(pieces)
    if last is None:
        shapes += [jax.ShapeDtypeStruct((n // 2, wide), F32)] * 2
    else:
        shapes.append(jax.ShapeDtypeStruct((wide, n), last))
    kernel = functools.partial(next_kernel, depth, len(xts), len(totals), len(pieces), block, last is not None)
    out = whole(kernel, shapes, *xts, *totals, *pieces, flops=2 * n * f * len(pieces) * (depth + wide), weight=0.5 if last is None else 1)
    return out[: len(pieces)], out[len(pieces) :]


def spread_kernel(own_ref, got_ref, keep_ref, *send_refs):
    n = keep_ref.shape[1]
    total = own_ref[...] + got_ref[...].astype(F32)
    keep_ref[...] = total[:, :n]
    for j, ref in enumerate(send_refs):
        ref[...] = total[:, (j + 1) * n : (j + 2) * n].astype(BF16)


def curve_kernel(classes, keep_ref, *refs):
    got_refs, p_ref, c_ref = refs[:-2], refs[-2], refs[-1]
    total = keep_ref[...]
    for ref in got_refs:
        total = total + ref[...].astype(F32)
    total = total[:classes, :]
    prob = p_ref[...].astype(F32)
    mixed = jnp.sum(prob * total, axis=0, keepdims=True)
    c_ref[:classes, :] = (prob * (total - mixed)).astype(BF16)
    c_ref[classes:, :] = jnp.zeros((c_ref.shape[0] - classes, c_ref.shape[1]), BF16)


def share_kernel(count, start, skip, block, halves, outs, seeded, *refs):
    left_refs, f_refs, o_refs = refs[:count], refs[count:-outs], refs[-outs:]
    seed_ref, f_refs = (f_refs[0], f_refs[1:]) if seeded else (None, f_refs)
    each = len(f_refs) // halves
    f = f_refs[0].shape[1]
    for h in range(halves):
        f_blocks = [(ref, at) for ref in f_refs[h * each : (h + 1) * each] for at in range(0, ref.shape[0], block)]
        total = seed_ref[:, h * f : (h + 1) * f] if seeded else None
        for left_ref, (f_ref, at) in zip(left_refs, f_blocks[start : start + count], strict=True):
            part = jnp.dot(left_ref[skip:, :], f_ref[at : at + block, :], preferred_element_type=F32)
            total = part if total is None else total + part
        if outs == 1:
            o_refs[0][:, h * f : (h + 1) * f] = total.astype(o_refs[0].dtype)
        else:
            for j in range(outs // halves):
                wide = f * halves // outs
                o_refs[h * (outs // halves) + j][...] = total[:, j * wide : (j + 1) * wide].astype(o_refs[0].dtype)


def add_kernel(*refs):
    total = refs[0][...].astype(F32)
    for ref in refs[1:-1]:
        total = total + ref[...].astype(F32)
    refs[-1][...] = total.astype(refs[-1].dtype)


def make_share(lefts, skip, feats, dtype, start=0, seed=None, outs=1):
    block = lefts[0].shape[1]
    wide, n, f = lefts[0].shape[0] - skip, block * len(lefts), sum(h[0].shape[1] for h in feats)
    shapes = [jax.ShapeDtypeStruct((wide, f // outs), dtype)] * outs
    return whole(
        functools.partial(share_kernel, len(lefts), start, skip, block, len(feats), outs, seed is not None),
        shapes if outs > 1 else shapes[0],
        *lefts, *([] if seed is None else [seed]), *[a for h in feats for a in h], flops=2 * n * f * wide,
    )


def whole(kernel, shapes, *args, flops=0, weight=1):
    size = sum(math.prod(a.shape) * a.dtype.itemsize for a in args)
    cost = pl.CostEstimate(flops=int(weight * flops), bytes_accessed=int(weight * size), transcendentals=0)
    return pl.pallas_call(kernel, out_shape=shapes, compiler_params=params(), cost_estimate=cost)(*args)


def on_device(line, ys, xs, inputs, probs, labels, proj_weight, phase, direction, damping):
    raw, own = inputs.shape
    classes = probs.shape[0]
    width = proj_weight.shape[1]
    depth = up(raw + 1, 16)
    wide = up(classes, 8)

    def swap_core(a):
        return lax.ppermute(a, "feat", [(i, i ^ 1) for i in range(2 * xs * ys)])

    def along(a, k):
        def to(i):
            return i ^ abs(k) if line & (line - 1) == 0 else (i + k) % line

        return lax.ppermute(a, "samp", [(i, to(i)) for i in range(line)])

    places = (1, 2, 3) if line == 4 else range(1, line)

    def across(a, dy, dx):
        def to(i):
            y, x, c = i // (2 * xs), i // 2 % xs, i % 2
            return ((y + dy) % ys * xs + (x + dx) % xs) * 2 + c

        return lax.ppermute(a, "feat", [(i, to(i)) for i in range(2 * xs * ys)])

    offsets = [(dy, dx) for dy in range(ys) for dx in range(xs)]
    rows, half = depth + wide, width // 2
    w_own = jnp.concatenate(
        [
            proj_weight,
            jnp.pad(phase, ((0, depth - raw - 1), (0, 0))),
            jnp.pad(direction, ((0, wide - classes), (0, 0))),
        ]
    )
    ws = {(0, dx): across(w_own, 0, dx) for dx in range(1, xs)}
    ws.update({(dy, 0): across(w_own, dy, 0) for dy in range(1, ys)})
    far = [(dy, dx) for dy in range(1, ys) for dx in range(1, xs)]
    halves = {}
    for dy, dx in far:
        halves[dy, dx] = [across(ws[0, dx][:, :half], dy, 0), across(ws[dy, 0][:, half:], 0, dx)]
    onehot = lax.broadcasted_iota(jnp.int32, probs.shape, 0) == labels[None, :]
    resid = (probs.astype(F32) - onehot.astype(F32)).astype(BF16)
    x_own = jnp.concatenate(
        [
            inputs,
            jnp.ones((1, own), BF16),
            jnp.zeros((depth - raw - 1, own), BF16),
            jnp.pad(resid, ((0, wide - classes), (0, 0))),
        ]
    )
    x_line = [x_own] + [along(x_own, k) for k in places]

    feats = {at: [[]] for at in offsets}
    xts, totals = [], []

    def first(some):
        n = own * len(some)
        xt, total, *part = whole(
            functools.partial(first_kernel, depth, len(some), 1),
            [jax.ShapeDtypeStruct((n, depth), BF16), jax.ShapeDtypeStruct((n, wide), F32)]
            + [jax.ShapeDtypeStruct((n, width), BF16)],
            *some, w_own, flops=2 * n * width * (depth + wide),
        )
        xts.append(xt)
        totals.append(total)
        feats[0, 0][0] += part

    for k in range(line):
        first(x_line[k : k + 1])
        if k + 1 < line:
            x_line[k + 1], totals[k] = lax.optimization_barrier((x_line[k + 1], totals[k]))
    x_peer = [swap_core(a) for a in x_line]
    first(x_peer)
    blocks = x_line + x_peer
    near = list(ws)
    got, totals = make_next(xts, totals, [ws[at] for at in near], depth, wide, own)
    for at, piece in zip(near, got, strict=True):
        feats[at] = [[piece]]

    def share(at, lefts, skip):
        return make_share(lefts, skip, feats[at], F32 if at == (0, 0) else BF16)

    def home(at, part):
        return across(part, -at[0], -at[1])

    parts = {at: share(at, blocks, depth) for at in near}
    totals, parts = lax.optimization_barrier((totals, parts))
    arrived = {at: home(at, parts[at]) for at in near}
    turned = []
    pieces = [w for at in far for w in halves[at]]
    for some, total, dtype in ((xts[-1:], totals[1], BF16), (xts[:-1], totals[0], F32)):
        got, (out,) = make_next(some, [total], pieces, depth, wide, own, dtype)
        turned.append((got, out))
    for j, at in enumerate(far):
        feats[at] = [[turned[1][0][2 * j + h], turned[0][0][2 * j + h]] for h in (0, 1)]
    t_other, t_own = turned[0][1], turned[1][1]
    t_got = swap_core(t_other)
    keep, *send = whole(
        spread_kernel,
        [jax.ShapeDtypeStruct((wide, own), F32)] + [jax.ShapeDtypeStruct((wide, own), BF16)] * (line - 1),
        t_own, t_got,
    )
    got = [along(a, -k) for k, a in zip(places, send, strict=True)]

    def collect(parts, some):
        out = parts[0, 0]
        for dy, dx in some:
            out = out + parts[dy, dx].astype(F32)
        return out[:classes]

    parts[0, 0] = share((0, 0), blocks, depth)
    keep, parts = lax.optimization_barrier((keep, parts))
    got, after = lax.optimization_barrier((got, blocks))
    parts.update({at: share(at, after, depth) for at in far})
    arrived.update({at: home(at, parts[at]) for at in far})
    curv = whole(
        functools.partial(curve_kernel, classes), jax.ShapeDtypeStruct((wide, own), BF16), keep, *got, probs
    )
    c_line = [curv] + [along(curv, k) for k in places]
    c_peer = [swap_core(a) for a in c_line]
    c_peer, ready = lax.optimization_barrier((c_peer, {at: arrived[at] for at in near}))
    seeds = {at: make_share(c_line, 0, feats[at], F32) for at in offsets[::-1]}

    def total_share(at, dtype, outs=1):
        return make_share(c_peer, 0, feats[at], dtype, line, seeds[at], outs)

    thirds = {at: total_share(at, BF16, 2) for at in far}
    c_peer, thirds = lax.optimization_barrier((c_peer, thirds))
    first_half = {(dy, dx): across(thirds[dy, dx][0], 0, -dx) for dy, dx in far}
    second_half = {(dy, dx): across(thirds[dy, dx][1], -dy, 0) for dy, dx in far}
    rest = {at: arrived[at] for at in far}
    first_half, second_half, rest = lax.optimization_barrier((first_half, second_half, rest))
    arrived = {**ready, **rest}
    gradient = collect({(0, 0): parts[0, 0], **arrived}, offsets[1:])
    hess = total_share((0, 0), F32)
    sides = [hess[:classes, :half], hess[:classes, half:]]
    for at in near:
        h = 0 if at[0] else 1
        plain = total_share(at, BF16, 2)
        others = [first_half[f] if at[0] else second_half[f] for f in far if at[0] in (0, f[0]) and at[1] in (0, f[1])]
        mixed = whole(add_kernel, jax.ShapeDtypeStruct(plain[h].shape, BF16), plain[h], *others)
        for side, piece in ((1 - h, home(at, plain[1 - h])), (h, home(at, mixed))):
            sides[side] = sides[side] + piece[:classes].astype(F32)
    hess_vec = jnp.concatenate(sides, axis=1) + damping[0] * direction.astype(F32)
    return (hess_vec, gradient)


def solution(mesh):
    line, feat = mesh.shape["samp"], mesh.shape["feat"]
    ys = 2 if feat % 4 == 0 else 1
    xs = feat // (2 * ys)
    placed = (
        P(None, ("samp", "feat")),
        P(None, ("samp", "feat")),
        P(("samp", "feat")),
        P(None, ("feat", "samp")),
        P(None, ("feat", "samp")),
        P(None, ("feat", "samp")),
        P(),
    )
    return jax.shard_map(
        functools.partial(on_device, line, ys, xs),
        mesh=mesh,
        in_specs=placed,
        out_specs=(P(None, ("feat", "samp")), P(None, ("feat", "samp"))),
        check_vma=False,
    )
```

```python
import functools
import math

import jax
import jax.numpy as jnp
from jax import lax
from jax.experimental import pallas as pl
from jax.experimental.pallas import tpu as pltpu
from jax.sharding import PartitionSpec as P

F32, BF16 = jnp.float32, jnp.bfloat16
VMEM = 16 * 2**20
COEFS = (0.99995902, -19.73094237, 64.67144178, -82.39080631, 45.6210511)
ROUNDER = 12582912.0


def up(value, step):
    return -(-value // step) * step


def params():
    return pltpu.CompilerParams(vmem_limit_bytes=VMEM)


def cosine(angle):
    turns = angle * (0.5 / math.pi)
    rest = turns - jnp.round(turns)
    square = rest * rest
    total = square * COEFS[-1] + COEFS[-2]
    for coef in COEFS[-3::-1]:
        total = total * square + coef
    return total


def fetch(refs, bufs, sems):
    copies = [pltpu.make_async_copy(ref, buf, sems.at[j]) for j, (ref, buf) in enumerate(zip(refs, bufs, strict=True))]
    for copy in copies:
        copy.start()
    for copy in copies:
        copy.wait()


def pack_weights_kernel(raw, depth, classes, w_hbm, ph_hbm, d_hbm, *refs):
    o_refs, (w_ref, ph_ref, d_ref, sems) = refs[:-4], refs[-4:]
    fetch((w_hbm, ph_hbm, d_hbm), (w_ref, ph_ref, d_ref), sems)
    rows, f = o_refs[0].shape
    for j, o_ref in enumerate(o_refs):
        here = slice(j * f, (j + 1) * f)
        o_ref[:raw, :] = w_ref[:, here]
        head = lax.broadcasted_iota(jnp.int32, (depth - raw, f), 0) == 0
        o_ref[raw:depth, :] = jnp.where(head, ph_ref[:, here].astype(F32), 0.0).astype(BF16)
        o_ref[depth : depth + classes, :] = d_ref[:, here]
        o_ref[depth + classes :, :] = jnp.zeros((rows - depth - classes, f), BF16)


def pack_samples_kernel(raw, depth, classes, x_hbm, p_hbm, l_hbm, o_ref, x_ref, p_ref, l_ref, sems):
    fetch((x_hbm, p_hbm, l_hbm), (x_ref, p_ref, l_ref), sems)
    rows, n = o_ref.shape
    o_ref[:raw, :] = x_ref[...]
    head = lax.broadcasted_iota(jnp.int32, (depth - raw, n), 0) == 0
    o_ref[raw:depth, :] = jnp.where(head, 1.0, 0.0).astype(BF16)
    ids = lax.broadcasted_iota(jnp.int32, (classes, n), 0)
    onehot = (ids == l_ref[...]).astype(F32)
    o_ref[depth : depth + classes, :] = (p_ref[...].astype(F32) - onehot).astype(BF16)
    o_ref[depth + classes :, :] = jnp.zeros((rows - depth - classes, n), BF16)


def pack(kernel, shapes, *args):
    return pl.pallas_call(
        kernel,
        in_specs=[pl.BlockSpec(memory_space=pltpu.HBM)] * len(args),
        out_shape=shapes,
        scratch_shapes=[pltpu.VMEM(a.shape, a.dtype) for a in args] + [pltpu.SemaphoreType.DMA((len(args),))],
        compiler_params=params(),
    )(*args)


def one_block(xt, w_ref, depth):
    feats = cosine(jnp.dot(xt, w_ref[:depth, :], preferred_element_type=F32)).astype(BF16)
    dims = (((1,), (1,)), ((), ()))
    return feats, lax.dot_general(feats, w_ref[depth:, :], dims, preferred_element_type=F32)


def first_kernel(depth, count, parts, *refs):
    x_refs, w_refs = refs[:count], refs[count : count + parts]
    xt_ref, t_ref, *f_refs = refs[count + parts :]
    n = x_refs[0].shape[1]
    for j in range(count):
        here = slice(j * n, (j + 1) * n)
        xt = x_refs[j][:depth, :].T
        xt_ref[here, :] = xt
        total = None
        for w_ref, f_ref in zip(w_refs, f_refs, strict=True):
            f_ref[here, :], tangent = one_block(xt, w_ref, depth)
            total = tangent if total is None else total + tangent
        t_ref[here, :] = total


def rows_of(refs, block, group):
    pieces = [(ref, at) for ref in refs for at in range(0, ref.shape[0], block)]
    return [pieces[j : j + group] for j in range(0, len(pieces), group)]


def load(pieces, block):
    (first, start), (_, end) = pieces[0], pieces[-1]
    if all(ref is first for ref, _ in pieces):
        return first[start : end + block, :]
    return jnp.concatenate([ref[at : at + block, :] for ref, at in pieces], axis=0)


def next_kernel(depth, count, totals, parts, block, last, *refs):
    xt_refs, t_refs = refs[:count], refs[count : count + totals]
    refs = refs[count + totals :]
    w_refs, f_refs, out_refs = refs[:parts], refs[parts : 2 * parts], refs[2 * parts :]
    spot = 0
    for xt_pieces, t_pieces in zip(rows_of(xt_refs, block, 2), rows_of(t_refs, block, 2), strict=True):
        xt, total = load(xt_pieces, block), load(t_pieces, block)
        n = xt.shape[0]
        for w_ref, f_ref in zip(w_refs, f_refs, strict=True):
            f_ref[spot : spot + n, :], tangent = one_block(xt, w_ref, depth)
            total = total + tangent
        if not last:
            here = spot % out_refs[0].shape[0]
            out_refs[spot // out_refs[0].shape[0]][here : here + n, :] = total
        else:
            out_refs[0][:, spot : spot + n] = total.T.astype(out_refs[0].dtype)
        spot += n


def make_next(xts, totals, pieces, depth, wide, block, last=None):
    n, f = sum(a.shape[0] for a in xts), pieces[0].shape[1]
    shapes = [jax.ShapeDtypeStruct((n, f), BF16)] * len(pieces)
    if last is None:
        shapes += [jax.ShapeDtypeStruct((n // 2, wide), F32)] * 2
    else:
        shapes.append(jax.ShapeDtypeStruct((wide, n), last))
    kernel = functools.partial(next_kernel, depth, len(xts), len(totals), len(pieces), block, last is not None)
    out = whole(kernel, shapes, *xts, *totals, *pieces, flops=2 * n * f * len(pieces) * (depth + wide), weight=0.5 if last is None else 1)
    return out[: len(pieces)], out[len(pieces) :]


def spread_kernel(own_ref, got_ref, keep_ref, *send_refs):
    n = keep_ref.shape[1]
    total = own_ref[...] + got_ref[...].astype(F32)
    keep_ref[...] = total[:, :n]
    for j, ref in enumerate(send_refs):
        ref[...] = total[:, (j + 1) * n : (j + 2) * n].astype(BF16)


def curve_kernel(classes, keep_ref, *refs):
    got_refs, p_ref, c_ref = refs[:-2], refs[-2], refs[-1]
    total = keep_ref[...]
    for ref in got_refs:
        total = total + ref[...].astype(F32)
    total = total[:classes, :]
    prob = p_ref[...].astype(F32)
    mixed = jnp.sum(prob * total, axis=0, keepdims=True)
    c_ref[:classes, :] = (prob * (total - mixed)).astype(BF16)
    c_ref[classes:, :] = jnp.zeros((c_ref.shape[0] - classes, c_ref.shape[1]), BF16)


def share_kernel(count, start, skip, block, halves, outs, seeded, *refs):
    left_refs, f_refs, o_refs = refs[:count], refs[count:-outs], refs[-outs:]
    seed_ref, f_refs = (f_refs[0], f_refs[1:]) if seeded else (None, f_refs)
    each = len(f_refs) // halves
    f = f_refs[0].shape[1]
    for h in range(halves):
        f_blocks = [(ref, at) for ref in f_refs[h * each : (h + 1) * each] for at in range(0, ref.shape[0], block)]
        total = seed_ref[:, h * f : (h + 1) * f] if seeded else None
        for left_ref, (f_ref, at) in zip(left_refs, f_blocks[start : start + count], strict=True):
            part = jnp.dot(left_ref[skip:, :], f_ref[at : at + block, :], preferred_element_type=F32)
            total = part if total is None else total + part
        if outs == 1:
            o_refs[0][:, h * f : (h + 1) * f] = total.astype(o_refs[0].dtype)
        else:
            for j in range(outs // halves):
                wide = f * halves // outs
                o_refs[h * (outs // halves) + j][...] = total[:, j * wide : (j + 1) * wide].astype(o_refs[0].dtype)


def add_kernel(*refs):
    total = refs[0][...].astype(F32)
    for ref in refs[1:-1]:
        total = total + ref[...].astype(F32)
    refs[-1][...] = total.astype(refs[-1].dtype)


def make_share(lefts, skip, feats, dtype, start=0, seed=None, outs=1):
    block = lefts[0].shape[1]
    wide, n, f = lefts[0].shape[0] - skip, block * len(lefts), sum(h[0].shape[1] for h in feats)
    shapes = [jax.ShapeDtypeStruct((wide, f // outs), dtype)] * outs
    return whole(
        functools.partial(share_kernel, len(lefts), start, skip, block, len(feats), outs, seed is not None),
        shapes if outs > 1 else shapes[0],
        *lefts, *([] if seed is None else [seed]), *[a for h in feats for a in h], flops=2 * n * f * wide,
    )


def whole(kernel, shapes, *args, flops=0, weight=1):
    size = sum(math.prod(a.shape) * a.dtype.itemsize for a in args)
    cost = pl.CostEstimate(flops=int(weight * flops), bytes_accessed=int(weight * size), transcendentals=0)
    return pl.pallas_call(kernel, out_shape=shapes, compiler_params=params(), cost_estimate=cost)(*args)


def on_device(line, ys, xs, inputs, probs, labels, proj_weight, phase, direction, damping):
    raw, own = inputs.shape
    classes = probs.shape[0]
    width = proj_weight.shape[1]
    depth = up(raw + 1, 16)
    wide = up(classes, 8)

    def swap_core(a):
        return lax.ppermute(a, "feat", [(i, i ^ 1) for i in range(2 * xs * ys)])

    def along(a, k):
        def to(i):
            return i ^ abs(k) if line & (line - 1) == 0 else (i + k) % line

        return lax.ppermute(a, "samp", [(i, to(i)) for i in range(line)])

    places = (2, 1, 3) if line == 4 else range(1, line)

    def across(a, dy, dx):
        def to(i):
            y, x, c = i // (2 * xs), i // 2 % xs, i % 2
            return ((y + dy) % ys * xs + (x + dx) % xs) * 2 + c

        return lax.ppermute(a, "feat", [(i, to(i)) for i in range(2 * xs * ys)])

    offsets = [(dy, dx) for dy in range(ys) for dx in range(xs)]
    rows, half = depth + wide, width // 2
    w_own = jnp.concatenate(
        [
            proj_weight,
            jnp.pad(phase, ((0, depth - raw - 1), (0, 0))),
            jnp.pad(direction, ((0, wide - classes), (0, 0))),
        ]
    )
    ws = {(0, dx): across(w_own, 0, dx) for dx in range(1, xs)}
    ws.update({(dy, 0): across(w_own, dy, 0) for dy in range(1, ys)})
    far = [(dy, dx) for dy in range(1, ys) for dx in range(1, xs)]
    halves = {}
    for dy, dx in far:
        halves[dy, dx] = [across(ws[0, dx][:, :half], dy, 0), across(ws[dy, 0][:, half:], 0, dx)]
    onehot = lax.broadcasted_iota(jnp.int32, probs.shape, 0) == labels[None, :]
    resid = (probs.astype(F32) - onehot.astype(F32)).astype(BF16)
    x_own = jnp.concatenate(
        [
            inputs,
            jnp.ones((1, own), BF16),
            jnp.zeros((depth - raw - 1, own), BF16),
            jnp.pad(resid, ((0, wide - classes), (0, 0))),
        ]
    )
    x_line = [x_own] + [along(x_own, k) for k in places]

    feats = {at: [[]] for at in offsets}
    xts, totals = [], []

    def first(some):
        n = own * len(some)
        xt, total, *part = whole(
            functools.partial(first_kernel, depth, len(some), 1),
            [jax.ShapeDtypeStruct((n, depth), BF16), jax.ShapeDtypeStruct((n, wide), F32)]
            + [jax.ShapeDtypeStruct((n, width), BF16)],
            *some, w_own, flops=2 * n * width * (depth + wide),
        )
        xts.append(xt)
        totals.append(total)
        feats[0, 0][0] += part

    for k in range(line):
        first(x_line[k : k + 1])
        if k + 1 < line:
            x_line[k + 1], totals[k] = lax.optimization_barrier((x_line[k + 1], totals[k]))
    x_peer = [swap_core(a) for a in x_line]
    first(x_peer)
    blocks = x_line + x_peer
    near = list(ws)
    got, totals = make_next(xts, totals, [ws[at] for at in near], depth, wide, own)
    for at, piece in zip(near, got, strict=True):
        feats[at] = [[piece]]

    def share(at, lefts, skip):
        return make_share(lefts, skip, feats[at], F32 if at == (0, 0) else BF16)

    def home(at, part):
        return across(part, -at[0], -at[1])

    parts = {at: share(at, blocks, depth) for at in near}
    totals, parts = lax.optimization_barrier((totals, parts))
    arrived = {at: home(at, parts[at]) for at in near}
    turned = []
    pieces = [w for at in far for w in halves[at]]
    for some, total, dtype in ((xts[-1:], totals[1], BF16), (xts[:-1], totals[0], F32)):
        got, (out,) = make_next(some, [total], pieces, depth, wide, own, dtype)
        turned.append((got, out))
    for j, at in enumerate(far):
        feats[at] = [[turned[1][0][2 * j + h], turned[0][0][2 * j + h]] for h in (0, 1)]
    t_other, t_own = turned[0][1], turned[1][1]
    t_got = swap_core(t_other)
    keep, *send = whole(
        spread_kernel,
        [jax.ShapeDtypeStruct((wide, own), F32)] + [jax.ShapeDtypeStruct((wide, own), BF16)] * (line - 1),
        t_own, t_got,
    )
    got = [along(a, -k) for k, a in zip(places, send, strict=True)]

    def collect(parts, some):
        out = parts[0, 0]
        for dy, dx in some:
            out = out + parts[dy, dx].astype(F32)
        return out[:classes]

    parts[0, 0] = share((0, 0), blocks, depth)
    keep, parts = lax.optimization_barrier((keep, parts))
    got, after = lax.optimization_barrier((got, blocks))
    parts.update({at: share(at, after, depth) for at in far})
    arrived.update({at: home(at, parts[at]) for at in far})
    curv = whole(
        functools.partial(curve_kernel, classes), jax.ShapeDtypeStruct((wide, own), BF16), keep, *got, probs
    )
    c_line = [curv] + [along(curv, k) for k in places]
    c_peer = [swap_core(a) for a in c_line]
    c_peer, ready = lax.optimization_barrier((c_peer, {at: arrived[at] for at in near}))
    seeds = {at: make_share(c_line, 0, feats[at], F32) for at in offsets[::-1]}

    def total_share(at, dtype, outs=1):
        return make_share(c_peer, 0, feats[at], dtype, line, seeds[at], outs)

    thirds = {at: total_share(at, BF16, 2) for at in far}
    c_peer, thirds = lax.optimization_barrier((c_peer, thirds))
    first_half = {(dy, dx): across(thirds[dy, dx][0], 0, -dx) for dy, dx in far}
    second_half = {(dy, dx): across(thirds[dy, dx][1], -dy, 0) for dy, dx in far}
    rest = {at: arrived[at] for at in far}
    first_half, second_half, rest = lax.optimization_barrier((first_half, second_half, rest))
    arrived = {**ready, **rest}
    gradient = collect({(0, 0): parts[0, 0], **arrived}, offsets[1:])
    hess = total_share((0, 0), F32)
    sides = [hess[:classes, :half], hess[:classes, half:]]
    for at in near:
        h = 0 if at[0] else 1
        plain = total_share(at, BF16, 2)
        others = [first_half[f] if at[0] else second_half[f] for f in far if at[0] in (0, f[0]) and at[1] in (0, f[1])]
        mixed = whole(add_kernel, jax.ShapeDtypeStruct(plain[h].shape, BF16), plain[h], *others)
        for side, piece in ((1 - h, home(at, plain[1 - h])), (h, home(at, mixed))):
            sides[side] = sides[side] + piece[:classes].astype(F32)
    hess_vec = jnp.concatenate(sides, axis=1) + damping[0] * direction.astype(F32)
    return (hess_vec, gradient)


def solution(mesh):
    line, feat = mesh.shape["samp"], mesh.shape["feat"]
    ys = 2 if feat % 4 == 0 else 1
    xs = feat // (2 * ys)
    placed = (
        P(None, ("samp", "feat")),
        P(None, ("samp", "feat")),
        P(("samp", "feat")),
        P(None, ("feat", "samp")),
        P(None, ("feat", "samp")),
        P(None, ("feat", "samp")),
        P(),
    )
    return jax.shard_map(
        functools.partial(on_device, line, ys, xs),
        mesh=mesh,
        in_specs=placed,
        out_specs=(P(None, ("feat", "samp")), P(None, ("feat", "samp"))),
        check_vma=False,
    )
```

```python
import functools
import math

import jax
import jax.numpy as jnp
from jax import lax
from jax.experimental import pallas as pl
from jax.experimental.pallas import tpu as pltpu
from jax.sharding import PartitionSpec as P

F32, BF16 = jnp.float32, jnp.bfloat16
VMEM = 16 * 2**20
COEFS = (0.99995902, -19.73094237, 64.67144178, -82.39080631, 45.6210511)
ROUNDER = 12582912.0


def up(value, step):
    return -(-value // step) * step


def params():
    return pltpu.CompilerParams(vmem_limit_bytes=VMEM)


def cosine(angle):
    turns = angle * (0.5 / math.pi)
    rest = turns - jnp.round(turns)
    square = rest * rest
    total = square * COEFS[-1] + COEFS[-2]
    for coef in COEFS[-3::-1]:
        total = total * square + coef
    return total


def fetch(refs, bufs, sems):
    copies = [pltpu.make_async_copy(ref, buf, sems.at[j]) for j, (ref, buf) in enumerate(zip(refs, bufs, strict=True))]
    for copy in copies:
        copy.start()
    for copy in copies:
        copy.wait()


def pack_weights_kernel(raw, depth, classes, w_hbm, ph_hbm, d_hbm, *refs):
    o_refs, (w_ref, ph_ref, d_ref, sems) = refs[:-4], refs[-4:]
    fetch((w_hbm, ph_hbm, d_hbm), (w_ref, ph_ref, d_ref), sems)
    rows, f = o_refs[0].shape
    for j, o_ref in enumerate(o_refs):
        here = slice(j * f, (j + 1) * f)
        o_ref[:raw, :] = w_ref[:, here]
        head = lax.broadcasted_iota(jnp.int32, (depth - raw, f), 0) == 0
        o_ref[raw:depth, :] = jnp.where(head, ph_ref[:, here].astype(F32), 0.0).astype(BF16)
        o_ref[depth : depth + classes, :] = d_ref[:, here]
        o_ref[depth + classes :, :] = jnp.zeros((rows - depth - classes, f), BF16)


def pack_samples_kernel(raw, depth, classes, x_hbm, p_hbm, l_hbm, o_ref, x_ref, p_ref, l_ref, sems):
    fetch((x_hbm, p_hbm, l_hbm), (x_ref, p_ref, l_ref), sems)
    rows, n = o_ref.shape
    o_ref[:raw, :] = x_ref[...]
    head = lax.broadcasted_iota(jnp.int32, (depth - raw, n), 0) == 0
    o_ref[raw:depth, :] = jnp.where(head, 1.0, 0.0).astype(BF16)
    ids = lax.broadcasted_iota(jnp.int32, (classes, n), 0)
    onehot = (ids == l_ref[...]).astype(F32)
    o_ref[depth : depth + classes, :] = (p_ref[...].astype(F32) - onehot).astype(BF16)
    o_ref[depth + classes :, :] = jnp.zeros((rows - depth - classes, n), BF16)


def pack(kernel, shapes, *args):
    return pl.pallas_call(
        kernel,
        in_specs=[pl.BlockSpec(memory_space=pltpu.HBM)] * len(args),
        out_shape=shapes,
        scratch_shapes=[pltpu.VMEM(a.shape, a.dtype) for a in args] + [pltpu.SemaphoreType.DMA((len(args),))],
        compiler_params=params(),
    )(*args)


def one_block(xt, w_ref, depth):
    feats = cosine(jnp.dot(xt, w_ref[:depth, :], preferred_element_type=F32)).astype(BF16)
    dims = (((1,), (1,)), ((), ()))
    return feats, lax.dot_general(feats, w_ref[depth:, :], dims, preferred_element_type=F32)


def first_kernel(depth, count, parts, *refs):
    x_refs, w_refs = refs[:count], refs[count : count + parts]
    xt_ref, t_ref, *f_refs = refs[count + parts :]
    n = x_refs[0].shape[1]
    group = 2 if count % 2 == 0 else 1
    for j in range(0, count, group):
        here = slice(j * n, (j + group) * n)
        for i in range(j, j + group):
            xt_ref[i * n : (i + 1) * n, :] = x_refs[i][:depth, :].T
        total = None
        for w_ref, f_ref in zip(w_refs, f_refs, strict=True):
            f_ref[here, :], tangent = one_block(xt_ref[here, :], w_ref, depth)
            total = tangent if total is None else total + tangent
        t_ref[here, :] = total


def rows_of(refs, block, group):
    pieces = [(ref, at) for ref in refs for at in range(0, ref.shape[0], block)]
    return [pieces[j : j + group] for j in range(0, len(pieces), group)]


def load(pieces, block):
    (first, start), (_, end) = pieces[0], pieces[-1]
    if all(ref is first for ref, _ in pieces):
        return first[start : end + block, :]
    return jnp.concatenate([ref[at : at + block, :] for ref, at in pieces], axis=0)


def next_kernel(depth, count, totals, parts, block, last, *refs):
    xt_refs, t_refs = refs[:count], refs[count : count + totals]
    refs = refs[count + totals :]
    w_refs, f_refs, out_refs = refs[:parts], refs[parts : 2 * parts], refs[2 * parts :]
    spot = 0
    for xt_pieces, t_pieces in zip(rows_of(xt_refs, block, 2), rows_of(t_refs, block, 2), strict=True):
        xt, total = load(xt_pieces, block), load(t_pieces, block)
        n = xt.shape[0]
        for w_ref, f_ref in zip(w_refs, f_refs, strict=True):
            f_ref[spot : spot + n, :], tangent = one_block(xt, w_ref, depth)
            total = total + tangent
        if not last:
            here = spot % out_refs[0].shape[0]
            out_refs[spot // out_refs[0].shape[0]][here : here + n, :] = total
        else:
            out_refs[0][:, spot : spot + n] = total.T.astype(out_refs[0].dtype)
        spot += n


def make_next(xts, totals, pieces, depth, wide, block, last=None):
    n, f = sum(a.shape[0] for a in xts), pieces[0].shape[1]
    shapes = [jax.ShapeDtypeStruct((n, f), BF16)] * len(pieces)
    if last is None:
        shapes += [jax.ShapeDtypeStruct((n // 2, wide), F32)] * 2
    else:
        shapes.append(jax.ShapeDtypeStruct((wide, n), last))
    kernel = functools.partial(next_kernel, depth, len(xts), len(totals), len(pieces), block, last is not None)
    out = whole(kernel, shapes, *xts, *totals, *pieces, flops=2 * n * f * len(pieces) * (depth + wide), weight=0.5)
    return out[: len(pieces)], out[len(pieces) :]


def spread_kernel(own_ref, got_ref, keep_ref, *send_refs):
    n = keep_ref.shape[1]
    total = own_ref[...] + got_ref[...].astype(F32)
    keep_ref[...] = total[:, :n]
    for j, ref in enumerate(send_refs):
        ref[...] = total[:, (j + 1) * n : (j + 2) * n].astype(BF16)


def curve_kernel(classes, keep_ref, *refs):
    got_refs, p_ref, c_ref = refs[:-2], refs[-2], refs[-1]
    total = keep_ref[...]
    for ref in got_refs:
        total = total + ref[...].astype(F32)
    total = total[:classes, :]
    prob = p_ref[...].astype(F32)
    mixed = jnp.sum(prob * total, axis=0, keepdims=True)
    c_ref[:classes, :] = (prob * (total - mixed)).astype(BF16)
    c_ref[classes:, :] = jnp.zeros((c_ref.shape[0] - classes, c_ref.shape[1]), BF16)


def share_kernel(count, start, skip, block, halves, outs, seeded, *refs):
    left_refs, f_refs, o_refs = refs[:count], refs[count:-outs], refs[-outs:]
    seed_ref, f_refs = (f_refs[0], f_refs[1:]) if seeded else (None, f_refs)
    each = len(f_refs) // halves
    f = f_refs[0].shape[1]
    for h in range(halves):
        f_blocks = [(ref, at) for ref in f_refs[h * each : (h + 1) * each] for at in range(0, ref.shape[0], block)]
        total = seed_ref[:, h * f : (h + 1) * f] if seeded else None
        for left_ref, (f_ref, at) in zip(left_refs, f_blocks[start : start + count], strict=True):
            part = jnp.dot(left_ref[skip:, :], f_ref[at : at + block, :], preferred_element_type=F32)
            total = part if total is None else total + part
        if outs == 1:
            o_refs[0][:, h * f : (h + 1) * f] = total.astype(o_refs[0].dtype)
        else:
            for j in range(outs // halves):
                wide = f * halves // outs
                o_refs[h * (outs // halves) + j][...] = total[:, j * wide : (j + 1) * wide].astype(o_refs[0].dtype)


def add_kernel(*refs):
    total = refs[0][...].astype(F32)
    for ref in refs[1:-1]:
        total = total + ref[...].astype(F32)
    refs[-1][...] = total.astype(refs[-1].dtype)


def make_share(lefts, skip, feats, dtype, start=0, seed=None, outs=1):
    block = lefts[0].shape[1]
    wide, n, f = lefts[0].shape[0] - skip, block * len(lefts), sum(h[0].shape[1] for h in feats)
    shapes = [jax.ShapeDtypeStruct((wide, f // outs), dtype)] * outs
    return whole(
        functools.partial(share_kernel, len(lefts), start, skip, block, len(feats), outs, seed is not None),
        shapes if outs > 1 else shapes[0],
        *lefts, *([] if seed is None else [seed]), *[a for h in feats for a in h], flops=2 * n * f * wide,
    )


def whole(kernel, shapes, *args, flops=0, weight=1):
    size = sum(math.prod(a.shape) * a.dtype.itemsize for a in args)
    cost = pl.CostEstimate(flops=int(weight * flops), bytes_accessed=int(weight * size), transcendentals=0)
    return pl.pallas_call(kernel, out_shape=shapes, compiler_params=params(), cost_estimate=cost)(*args)


def on_device(line, ys, xs, inputs, probs, labels, proj_weight, phase, direction, damping):
    raw, own = inputs.shape
    classes = probs.shape[0]
    width = proj_weight.shape[1]
    depth = up(raw + 1, 16)
    wide = up(classes, 8)

    def swap_core(a):
        return lax.ppermute(a, "feat", [(i, i ^ 1) for i in range(2 * xs * ys)])

    def along(a, k):
        def to(i):
            return i ^ abs(k) if line & (line - 1) == 0 else (i + k) % line

        return lax.ppermute(a, "samp", [(i, to(i)) for i in range(line)])

    places = (2, 1, 3) if line == 4 else range(1, line)

    def across(a, dy, dx):
        def to(i):
            y, x, c = i // (2 * xs), i // 2 % xs, i % 2
            return ((y + dy) % ys * xs + (x + dx) % xs) * 2 + c

        return lax.ppermute(a, "feat", [(i, to(i)) for i in range(2 * xs * ys)])

    offsets = [(dy, dx) for dy in range(ys) for dx in range(xs)]
    rows, half = depth + wide, width // 2
    w_own = jnp.concatenate(
        [
            proj_weight,
            jnp.pad(phase, ((0, depth - raw - 1), (0, 0))),
            jnp.pad(direction, ((0, wide - classes), (0, 0))),
        ]
    )
    ws = {(0, dx): across(w_own, 0, dx) for dx in range(1, xs)}
    ws.update({(dy, 0): across(w_own, dy, 0) for dy in range(1, ys)})
    far = [(dy, dx) for dy in range(1, ys) for dx in range(1, xs)]
    halves = {}
    for dy, dx in far:
        halves[dy, dx] = [across(ws[0, dx][:, :half], dy, 0), across(ws[dy, 0][:, half:], 0, dx)]
    onehot = lax.broadcasted_iota(jnp.int32, probs.shape, 0) == labels[None, :]
    resid = (probs.astype(F32) - onehot.astype(F32)).astype(BF16)
    x_own = jnp.concatenate(
        [
            inputs,
            jnp.ones((1, own), BF16),
            jnp.zeros((depth - raw - 1, own), BF16),
            jnp.pad(resid, ((0, wide - classes), (0, 0))),
        ]
    )
    x_line = [x_own] + [along(x_own, k) for k in places]

    feats = {at: [[]] for at in offsets}
    xts, totals = [], []

    def first(some):
        n = own * len(some)
        xt, total, *part = whole(
            functools.partial(first_kernel, depth, len(some), 1),
            [jax.ShapeDtypeStruct((n, depth), BF16), jax.ShapeDtypeStruct((n, wide), F32)]
            + [jax.ShapeDtypeStruct((n, width), BF16)],
            *some, w_own, flops=2 * n * width * (depth + wide),
        )
        xts.append(xt)
        totals.append(total)
        feats[0, 0][0] += part

    for k in range(line):
        first(x_line[k : k + 1])
        if k + 1 < line:
            x_line[k + 1], totals[k] = lax.optimization_barrier((x_line[k + 1], totals[k]))
    x_peer = [swap_core(a) for a in x_line]
    first(x_peer)
    blocks = x_line + x_peer
    near = list(ws)
    got, totals = make_next(xts, totals, [ws[at] for at in near], depth, wide, own)
    for at, piece in zip(near, got, strict=True):
        feats[at] = [[piece]]

    def share(at, lefts, skip):
        return make_share(lefts, skip, feats[at], F32 if at == (0, 0) else BF16)

    def home(at, part):
        return across(part, -at[0], -at[1])

    parts = {at: share(at, blocks, depth) for at in near}
    totals, parts = lax.optimization_barrier((totals, parts))
    arrived = {at: home(at, parts[at]) for at in near}
    turned = []
    pieces = [w for at in far for w in halves[at]]
    for some, total, dtype in ((xts[-1:], totals[1], BF16), (xts[:-1], totals[0], F32)):
        got, (out,) = make_next(some, [total], pieces, depth, wide, own, dtype)
        turned.append((got, out))
    for j, at in enumerate(far):
        feats[at] = [[turned[1][0][2 * j + h], turned[0][0][2 * j + h]] for h in (0, 1)]
    t_other, t_own = turned[0][1], turned[1][1]
    t_got = swap_core(t_other)
    keep, *send = whole(
        spread_kernel,
        [jax.ShapeDtypeStruct((wide, own), F32)] + [jax.ShapeDtypeStruct((wide, own), BF16)] * (line - 1),
        t_own, t_got,
    )
    got = [along(a, -k) for k, a in zip(places, send, strict=True)]

    def collect(parts, some):
        out = parts[0, 0]
        for dy, dx in some:
            out = out + parts[dy, dx].astype(F32)
        return out[:classes]

    parts[0, 0] = share((0, 0), blocks, depth)
    keep, parts = lax.optimization_barrier((keep, parts))
    got, after = lax.optimization_barrier((got, blocks))
    parts.update({at: share(at, after, depth) for at in far})
    arrived.update({at: home(at, parts[at]) for at in far})
    curv = whole(
        functools.partial(curve_kernel, classes), jax.ShapeDtypeStruct((wide, own), BF16), keep, *got, probs
    )
    c_line = [curv] + [along(curv, k) for k in places]
    c_peer = [swap_core(a) for a in c_line]
    c_peer, ready = lax.optimization_barrier((c_peer, {at: arrived[at] for at in near}))
    seeds = {at: make_share(c_line, 0, feats[at], F32) for at in offsets[::-1]}

    def total_share(at, dtype, outs=1):
        return make_share(c_peer, 0, feats[at], dtype, line, seeds[at], outs)

    thirds = {at: total_share(at, BF16, 2) for at in far}
    c_peer, thirds = lax.optimization_barrier((c_peer, thirds))
    first_half = {(dy, dx): across(thirds[dy, dx][0], 0, -dx) for dy, dx in far}
    second_half = {(dy, dx): across(thirds[dy, dx][1], -dy, 0) for dy, dx in far}
    rest = {at: arrived[at] for at in far}
    first_half, second_half, rest = lax.optimization_barrier((first_half, second_half, rest))
    arrived = {**ready, **rest}
    gradient = collect({(0, 0): parts[0, 0], **arrived}, offsets[1:])
    hess = total_share((0, 0), F32)
    sides = [hess[:classes, :half], hess[:classes, half:]]
    for at in near:
        h = 0 if at[0] else 1
        plain = total_share(at, BF16, 2)
        others = [first_half[f] if at[0] else second_half[f] for f in far if at[0] in (0, f[0]) and at[1] in (0, f[1])]
        mixed = whole(add_kernel, jax.ShapeDtypeStruct(plain[h].shape, BF16), plain[h], *others)
        for side, piece in ((1 - h, home(at, plain[1 - h])), (h, home(at, mixed))):
            sides[side] = sides[side] + piece[:classes].astype(F32)
    hess_vec = jnp.concatenate(sides, axis=1) + damping[0] * direction.astype(F32)
    return (hess_vec, gradient)


def solution(mesh):
    line, feat = mesh.shape["samp"], mesh.shape["feat"]
    ys = 2 if feat % 4 == 0 else 1
    xs = feat // (2 * ys)
    placed = (
        P(None, ("samp", "feat")),
        P(None, ("samp", "feat")),
        P(("samp", "feat")),
        P(None, ("feat", "samp")),
        P(None, ("feat", "samp")),
        P(None, ("feat", "samp")),
        P(),
    )
    return jax.shard_map(
        functools.partial(on_device, line, ys, xs),
        mesh=mesh,
        in_specs=placed,
        out_specs=(P(None, ("feat", "samp")), P(None, ("feat", "samp"))),
        check_vma=False,
    )
```
